256 devices in a mesh: group: 16 (over x, z_lo), fsdp: 16 (over z_hi, y, core).
Axes of the slice: x: 4, y: 4, z: 8 (z_hi: 2, z_lo: 4; z = z_hi * 4 + z_lo), core: 2. Of those that a mesh axis runs over, the one named last changes fastest.
Arguments:
- activations: bfloat16 [2, 16, 6144, 2560], P(None, 'group', 'fsdp'), may hold values from -6 to 6
- out_grads: bfloat16 [2, 16, 6144, 2560], P(None, 'group', 'fsdp'), may hold values from -0.078125 to 0.078125
- weight: bfloat16 [16, 2560, 2560], P('group', 'fsdp'), may hold values from -0.1 to 0.1
- first_moment: bfloat16 [16, 2560, 2560], P('group', 'fsdp'), may hold values from -0.2 to 0.2
- second_moment: bfloat16 [16, 2560, 2560], P('group', 'fsdp'), may hold values from 0.049804688 to 2
- step_index: int32 [1], replicated, may hold values from 0 to 63
Outputs:
- new_weight: bfloat16 [16, 2560, 2560], P('group', 'fsdp')
- new_moment: float32 [16, 2560, 2560], P('group', 'fsdp')
The draws below stay inside these ranges and needn't reach their ends.
All inputs are finite; a program needn't handle non-finite values.
Results may differ from the reference program's by a relative error of at most 0.018.
Values may be sent and summed in bfloat16 or wider, within the bound.
No kernel may reach another device: no remote copies, remote signals or barrier semaphores. Data moves between devices by JAX's collectives and lax.ppermute only.
A program may use at most 192 MiB of HBM per device.

```python
import math
import jax
import jax.numpy as jnp
from jax import lax

IN = 2560
OUT = 2560
TOK_DEV = 384
STEPS = 2
GROUPS = 16
TOKENS = 6144
N_GROUP = 16
N_FSDP = 16


def draw_weight(key, part):
    key = jax.random.fold_in(key, 11)
    values = 0.02 * jnp.clip(jax.random.normal(key, (GROUPS, IN, OUT), jnp.float32), -4.875, 4.875)
    return values.astype(jnp.bfloat16)


def draw_first_moment(key, part):
    key = jax.random.fold_in(key, 23)
    values = 0.04 * jnp.clip(jax.random.normal(key, (GROUPS, IN, OUT), jnp.float32), -4.875, 4.875)
    return values.astype(jnp.bfloat16)


def with_spikes(array, key, source, target, shards_of, factor):
    def block_of(axis_at):
        return (jnp.arange(array.shape[axis_at]) // (array.shape[axis_at] // shards_of)).reshape((-1,) + (1,) * (array.ndim - 1 - axis_at))

    one_side = jax.random.permutation(key, shards_of)[block_of(target)]
    second = (block_of(target) + shards_of // 2) % shards_of
    return jnp.where((block_of(source) == one_side) | (block_of(source) == second), factor * array, array)


def shard_levels(rng, extent, shards, least, top_value):
    gain = 1.0
    for position, shards_of in shards:
        draws = jax.random.uniform(jax.random.fold_in(jax.random.fold_in(rng, 6), position), (shards_of,), jnp.float32, least / len(shards), top_value / len(shards))
        gain = gain * jnp.repeat(jnp.exp(draws), extent[position] // shards_of).reshape((-1,) + (1,) * (len(extent) - 1 - position))
    return gain


def scatter_about(rng, extent, scale, limit, shards=(), kind=jnp.bfloat16):
    entries = jax.random.normal(rng, extent, jnp.float32) * scale
    if len(shards) > 0:
        entries = shard_levels(rng, extent, shards, -0.22, 0.18) * entries
    return jnp.clip(entries, min=-limit, max=limit).astype(kind)


def gaussian_with(key, dims, scale, reach, cuts, heavy, held_as=jnp.bfloat16):
    array = scale * jax.random.normal(key, dims, jnp.float32)
    if cuts:
        array = array * shard_levels(key, dims, cuts, -0.22, 0.18)
    return jnp.clip(with_spikes(array, jax.random.fold_in(key, 3), *heavy), -reach, reach).astype(held_as)


def setup_inputs(seed: int = 0) -> dict:
    splits = jax.random.split(jax.random.key(seed), 7)
    return {
        "activations": gaussian_with(splits[0], (STEPS, GROUPS, TOKENS, IN), 1.0, 6.0, ((1, 16), (2, 16)), (2, 3, 16, 2.0)),
        "out_grads": scatter_about(splits[1], (STEPS, GROUPS, TOKENS, OUT), TOKENS ** -0.5, 0.078125, ((1, 16), (2, 16))),
        "weight": draw_weight(jax.random.fold_in(splits[6], 71), 0),
        "first_moment": draw_first_moment(jax.random.fold_in(splits[6], 71), 0),
        "second_moment": jnp.clip(jnp.exp(math.log(2.0) - 3.6927934 * jax.random.uniform(splits[4], (GROUPS, IN, OUT), jnp.float32) ** shard_levels(splits[4], (GROUPS, IN, OUT), ((0, 16), (1, 16)), -0.2, 0.2)), 0.049804688, 2.0).astype(jnp.bfloat16),
        "step_index": jax.random.randint(splits[5], (1,), 0, 64).astype(jnp.int32),
    }


LEARN_RATE = 0.05
WEIGHT_DECAY = 0.1
BETA_ONE = 0.9
BETA_TWO = 0.95
EPSILON = 1e-08

def group_gradient(blocks):
    x_rows, y_rows = blocks
    x_rows = x_rows.reshape(N_FSDP, TOK_DEV, IN)
    y_rows = y_rows.reshape(N_FSDP, TOK_DEV, OUT)

    def accumulate(running, pair):
        x_block, y_block = pair
        partial_sum = jnp.dot(x_block.T, y_block, preferred_element_type=jnp.float32)
        return (running + partial_sum.astype(jnp.bfloat16).astype(jnp.float32), None)
    running, _ = lax.scan(accumulate, jnp.zeros((IN, OUT), jnp.float32), (x_rows, y_rows))
    return running

def reference(activations, out_grads, weight, first_moment, second_moment, step_index):
    params = weight.astype(jnp.float32)
    first_state = first_moment.astype(jnp.float32)
    second_state = second_moment.astype(jnp.float32)
    levels = N_GROUP.bit_length() - 1
    averaged = weight
    for section in range(2):
        gradient = lax.map(group_gradient, (activations[section], out_grads[section]))
        first_state = BETA_ONE * first_state + (1.0 - BETA_ONE) * gradient
        second_state = BETA_TWO * second_state + (1.0 - BETA_TWO) * gradient * gradient
        updated = params - LEARN_RATE * (first_state / (jnp.sqrt(second_state) + EPSILON) + WEIGHT_DECAY * params)
        rounded = updated.astype(jnp.bfloat16)
        distance = jnp.left_shift(jnp.int32(1), ((step_index[0] + section) % levels).astype(jnp.int32))
        partner = jnp.roll(rounded, distance, axis=0)
        averaged = ((rounded.astype(jnp.float32) + partner.astype(jnp.float32)) * 0.5).astype(jnp.bfloat16)
        params = averaged.astype(jnp.float32)
    return (averaged, first_state)
```

```python
from functools import partial

import jax
import jax.numpy as jnp
from jax import lax
from jax.experimental import pallas as pl
from jax.experimental.pallas import tpu as pltpu
from jax.sharding import PartitionSpec as P

LEARN_RATE = 0.05
WEIGHT_DECAY = 0.1
BETA_ONE = 0.9
BETA_TWO = 0.95
EPSILON = 1e-08

Z_HI, Y, CORES = 2, 4, 2
N_FSDP = Z_HI * Y * CORES
N_GROUP = 16
ROWS = 160
TOK = 384
WIDTH = 2560
CHUNKS = ((1280, 1280), (1024, 1024, 512))
VMEM = 48 * 1024 * 1024


def fsdp_move(block, move):
    def target(i):
        z, y, c = i // (Y * CORES), (i // CORES) % Y, i % CORES
        z, y, c = move(z, y, c)
        return ((z % Z_HI) * Y + y % Y) * CORES + c % CORES

    return lax.ppermute(block, "fsdp", [(i, target(i)) for i in range(N_FSDP)])


def y_move(block, shift):
    return fsdp_move(block, lambda z, y, c: (z, y + shift, c))


def z_swap(block):
    return fsdp_move(block, lambda z, y, c: (z + 1, y, c))


def core_swap(block):
    return fsdp_move(block, lambda z, y, c: (z, y, c + 1))


def group_move(block, distance):
    return lax.ppermute(
        block, "group", [((i - distance) % N_GROUP, i) for i in range(N_GROUP)]
    )


def turn_kernel(core_ref, x_ref, own_ref, other_ref, turned):
    for j in range(WIDTH // 128):
        turned[j * 128 : (j + 1) * 128, :] = x_ref[:, j * 128 : (j + 1) * 128].T
    core = core_ref[0]
    for b in range(Z_HI * Y):
        for ref, k in ((own_ref, core), (other_ref, 1 - core)):
            start = pl.multiple_of((b * CORES + k) * ROWS, ROWS)
            ref[b] = turned[pl.ds(start, ROWS), :]


def turn(core, x):
    shape = jax.ShapeDtypeStruct((Z_HI * Y, ROWS, TOK), jnp.bfloat16)
    return pl.pallas_call(
        turn_kernel,
        grid_spec=pltpu.PrefetchScalarGridSpec(
            num_scalar_prefetch=1,
            grid=(1,),
            in_specs=[pl.BlockSpec((TOK, WIDTH), lambda i, s: (0, 0))],
            out_specs=[pl.BlockSpec((Z_HI * Y, ROWS, TOK), lambda i, s: (0, 0, 0))] * 2,
            scratch_shapes=[pltpu.VMEM((WIDTH, TOK), jnp.bfloat16)],
        ),
        out_shape=[shape, shape],
        compiler_params=pltpu.CompilerParams(vmem_limit_bytes=VMEM),
        cost_estimate=pl.CostEstimate(flops=0, bytes_accessed=12 * 1024 * 1024, transcendentals=0),
    )(core, x)


def products_kernel(units, adds, blocks_ref, *refs):
    own, other = refs[:units], refs[units : 2 * units]
    y_own, y_other = refs[2 * units : 2 * units + 2]
    rest = refs[2 * units + 2 :]
    terms, outs = rest[: sum(adds)], rest[sum(adds) :]
    x_own = jnp.concatenate([r[0] for r in own], axis=0)
    x_other = jnp.concatenate([r[0] for r in other], axis=0)
    total = jnp.dot(x_own, y_own[...], preferred_element_type=jnp.float32)
    total += jnp.dot(x_other, y_other[...], preferred_element_type=jnp.float32)
    at = 0
    for u in range(units):
        part = total[u * ROWS : (u + 1) * ROWS]
        for _ in range(adds[u]):
            part = part + terms[at][...].astype(jnp.float32)
            at += 1
        outs[u][...] = part.astype(outs[u].dtype)


def products(blocks, pair, column, width, adds, dtypes):
    x_own, x_other, y_own, y_other = pair
    units = len(dtypes)
    terms = [t for per_unit in adds for t in per_unit]
    x_specs = [
        pl.BlockSpec((1, ROWS, TOK), lambda i, s, u=u: (s[u], 0, 0)) for u in range(units)
    ]
    y_spec = pl.BlockSpec((TOK, width), lambda i, s: (0, column // width))
    piece = pl.BlockSpec((ROWS, width), lambda i, s: (0, 0))
    return pl.pallas_call(
        partial(products_kernel, units, tuple(len(a) for a in adds)),
        grid_spec=pltpu.PrefetchScalarGridSpec(
            num_scalar_prefetch=1,
            grid=(1,),
            in_specs=x_specs * 2 + [y_spec] * 2 + [piece] * len(terms),
            out_specs=[piece] * units,
        ),
        out_shape=[jax.ShapeDtypeStruct((ROWS, width), d) for d in dtypes],
        compiler_params=pltpu.CompilerParams(vmem_limit_bytes=VMEM),
        cost_estimate=pl.CostEstimate(
            flops=2 * units * ROWS * 2 * TOK * width,
            bytes_accessed=2 * (2 * TOK * width + 2 * units * ROWS * TOK + 2 * units * ROWS * width),
            transcendentals=0,
        ),
    )(blocks, *([x_own] * units), *([x_other] * units), y_own, y_other, *terms)


def adam(params, first, second, gradient):
    first = BETA_ONE * first + (1.0 - BETA_ONE) * gradient
    second = BETA_TWO * second + (1.0 - BETA_TWO) * gradient * gradient
    updated = params - LEARN_RATE * (first / (jnp.sqrt(second) + EPSILON) + WEIGHT_DECAY * params)
    return first, second, updated.astype(jnp.bfloat16)


def averaged(own, partner):
    return ((own.astype(jnp.float32) + partner.astype(jnp.float32)) * 0.5).astype(jnp.bfloat16)


def both_steps(distances, x, y, weight, first, second):
    index = lax.axis_index("fsdp")
    core, at_y, at_z = index % CORES, (index // CORES) % Y, index // (Y * CORES)

    def block(dy, dz):
        return ((at_z + dz) % Z_HI) * Y + (at_y + dy) % Y

    def chosen(*pairs):
        return jnp.stack([block(*p) for p in pairs]).astype(jnp.int32)

    bf16, f32 = jnp.bfloat16, jnp.float32
    core = core.astype(jnp.int32)[None]
    pairs = []
    for s in range(2):
        x_own, x_give = turn(core, x[s, 0])
        pairs.append((x_own, core_swap(x_give), y[s, 0], core_swap(y[s, 0])))

    def reduced(s):
        result, column = [], 0
        for width in CHUNKS[s]:
            go = partial(products, pair=pairs[s], column=column, width=width)
            far_up, far_down, near_up, near_down = go(
                chosen((2, 0), (2, 1), (1, 1), (-1, 0)), adds=[()] * 4, dtypes=[bf16] * 4
            )
            far_up, far_down = y_move(far_up, 1), y_move(far_down, -1)
            near_up, near_down = y_move(near_up, 1), y_move(near_down, -1)
            sum_up, sum_down = go(
                chosen((1, 0), (-1, 1)), adds=[(far_up,), (far_down,)], dtypes=[bf16] * 2
            )
            sum_up, sum_down = y_move(sum_up, 1), y_move(sum_down, -1)
            mine, give = go(
                chosen((0, 0), (0, 1)),
                adds=[(sum_up, near_down), (near_up, sum_down)],
                dtypes=[f32, bf16],
            )
            result.append((mine, z_swap(give), column, width))
            column += width
        return result

    def cut(a, column, width):
        return a[:, column : column + width]

    w32 = weight[0].astype(f32)
    m32, v32 = first[0].astype(f32), second[0].astype(f32)
    state = []
    for mine, got, column, width in reduced(0):
        m, v, u = adam(
            cut(w32, column, width),
            cut(m32, column, width),
            cut(v32, column, width),
            mine + got.astype(f32),
        )
        state.append((m, v, averaged(u, group_move(u, distances[0]))))
    m, v, w = (jnp.concatenate(parts, axis=1) for parts in zip(*state))
    weights, moments = [], []
    for mine, got, column, width in reduced(1):
        m_new, _, u = adam(
            cut(w, column, width).astype(f32),
            cut(m, column, width),
            cut(v, column, width),
            mine + got.astype(f32),
        )
        weights.append(averaged(u, group_move(u, distances[1])))
        moments.append(m_new)
    return jnp.concatenate(weights, axis=1)[None], jnp.concatenate(moments, axis=1)[None]


def per_device(activations, out_grads, weight, first_moment, second_moment, step_index):
    levels = N_GROUP.bit_length() - 1
    branches = [
        partial(both_steps, (1 << level, 1 << ((level + 1) % levels))) for level in range(levels)
    ]
    return lax.switch(
        step_index[0] % levels,
        branches,
        activations,
        out_grads,
        weight,
        first_moment,
        second_moment,
    )


def solution(mesh):
    in_specs = (
        P(None, "group", "fsdp", None),
        P(None, "group", "fsdp", None),
        P("group", "fsdp", None),
        P("group", "fsdp", None),
        P("group", "fsdp", None),
        P(),
    )
    out_specs = (P("group", "fsdp", None), P("group", "fsdp", None))
    return jax.shard_map(
        per_device, mesh=mesh, in_specs=in_specs, out_specs=out_specs, check_vma=False
    )
```

```python
from functools import partial

import jax
import jax.numpy as jnp
from jax import lax
from jax.experimental import pallas as pl
from jax.experimental.pallas import tpu as pltpu
from jax.sharding import PartitionSpec as P

LEARN_RATE = 0.05
WEIGHT_DECAY = 0.1
BETA_ONE = 0.9
BETA_TWO = 0.95
EPSILON = 1e-08

Z_HI, Y, CORES = 2, 4, 2
N_FSDP = Z_HI * Y * CORES
N_GROUP = 16
ROWS = 160
TOK = 384
WIDTH = 2560
FIRST = ((0, 1536), (1536, 1024))
SECOND = ((0, 1024), (1024, 1024))
LAST = (2048, 512)
TILE = 256
HALF = ROWS // 2


def fsdp_move(block, move):
    def target(i):
        z, y, c = i // (Y * CORES), (i // CORES) % Y, i % CORES
        z, y, c = move(z, y, c)
        return ((z % Z_HI) * Y + y % Y) * CORES + c % CORES

    return lax.ppermute(block, "fsdp", [(i, target(i)) for i in range(N_FSDP)])


def y_move(block, shift):
    return fsdp_move(block, lambda z, y, c: (z, y + shift, c))


def z_swap(block):
    return fsdp_move(block, lambda z, y, c: (z + 1, y, c))


def core_swap(block):
    return fsdp_move(block, lambda z, y, c: (z, y, c + 1))


def group_move(block, distance):
    return lax.ppermute(
        block, "group", [((i - distance) % N_GROUP, i) for i in range(N_GROUP)]
    )


def turn_kernel(core_ref, x_ref, own_ref, other_ref, turned):
    def one(j, carry):
        at = pl.multiple_of(j * 256, 256)
        turned[pl.ds(at, 256), :] = x_ref[:, pl.ds(at, 256)].T
        return carry

    lax.fori_loop(0, WIDTH // 256, one, 0)
    core = core_ref[0]

    def give(b, carry):
        for ref, k in ((own_ref, core), (other_ref, 1 - core)):
            start = pl.multiple_of((b * CORES + k) * ROWS, ROWS)
            ref[b] = turned[pl.ds(start, ROWS), :]
        return carry

    lax.fori_loop(0, Z_HI * Y, give, 0)


def turn(core, x, step):
    shape = jax.ShapeDtypeStruct((Z_HI * Y, ROWS, TOK), jnp.bfloat16)
    return pl.pallas_call(
        turn_kernel,
        grid_spec=pltpu.PrefetchScalarGridSpec(
            num_scalar_prefetch=1,
            grid=(1,),
            in_specs=[pl.BlockSpec((None, None, TOK, WIDTH), lambda i, s: (step, 0, 0, 0))],
            out_specs=[pl.BlockSpec((Z_HI * Y, ROWS, TOK), lambda i, s: (0, 0, 0))] * 2,
            scratch_shapes=[pltpu.VMEM((WIDTH, TOK), jnp.bfloat16)],
        ),
        out_shape=[shape, shape],
        compiler_params=pltpu.CompilerParams(vmem_limit_bytes=16 * 1024 * 1024),
        cost_estimate=pl.CostEstimate(flops=0, bytes_accessed=6 * 1024 * 1024, transcendentals=0),
    )(core, x)


def products_kernel(adds, layout, terms, blocks_ref, *refs):
    units = len(adds)
    own, other = refs[:units], refs[units : 2 * units]
    y_own, y_other = refs[2 * units : 2 * units + 2]
    given = refs[2 * units + 2 : 2 * units + 2 + terms]
    outs = refs[len(refs) - len(layout) :]
    x = jnp.concatenate(
        [jnp.concatenate([a[0], b[0]], axis=1) for a, b in zip(own, other)], axis=0
    )
    y = jnp.concatenate([y_own[...], y_other[...]], axis=0)
    total = jnp.dot(x, y, preferred_element_type=jnp.float32)
    parts = []
    for u, per_unit in enumerate(adds):
        part = total[u * ROWS : (u + 1) * ROWS]
        for term, plane, low, high in per_unit:
            more = given[term][plane].astype(jnp.float32)
            if (low, high) == (0, ROWS):
                part = part + more
            elif low == 0:
                part = jnp.concatenate([part[:high] + more, part[high:]], axis=0)
            else:
                part = jnp.concatenate([part[:low], part[low:] + more], axis=0)
        parts.append(part)
    for out, planes in zip(outs, layout):
        for p, (u, low, high) in enumerate(planes):
            out[p] = parts[u][low:high].astype(out.dtype)


def products(pair, step, chunk, blocks, adds, terms, layout, dtypes, after=()):
    x_own, x_other, y_own, y_other = pair
    column, width = chunk
    units = len(adds)
    x_specs = [
        pl.BlockSpec((1, ROWS, TOK), lambda j, s, u=u: (s[u], 0, 0)) for u in range(units)
    ]
    y_spec = pl.BlockSpec(
        (None, None, TOK, TILE), lambda j, s: (step, 0, 0, column // TILE + j)
    )

    def piece(planes, rows):
        return pl.BlockSpec((planes, rows, TILE), lambda j, s: (0, 0, j))

    outs = [(len(planes), planes[0][2] - planes[0][1], width) for planes in layout]
    moved = sum(t.size for t in terms) + sum(p * r * w for p, r, w in outs)
    return pl.pallas_call(
        partial(products_kernel, adds, layout, len(terms)),
        grid_spec=pltpu.PrefetchScalarGridSpec(
            num_scalar_prefetch=1,
            grid=(width // TILE,),
            in_specs=x_specs * 2
            + [y_spec] * 2
            + [piece(*t.shape[:2]) for t in terms]
            + [pl.BlockSpec(memory_space=pl.ANY)] * len(after),
            out_specs=[piece(*o[:2]) for o in outs],
        ),
        out_shape=[jax.ShapeDtypeStruct(o, d) for o, d in zip(outs, dtypes)],
        compiler_params=pltpu.CompilerParams(vmem_limit_bytes=16 * 1024 * 1024),
        cost_estimate=pl.CostEstimate(
            flops=2 * units * ROWS * 2 * TOK * width,
            bytes_accessed=2 * (2 * TOK * width + 2 * units * ROWS * TOK + moved),
            transcendentals=0,
        ),
    )(blocks, *([x_own] * units), *([x_other] * units), y_own, y_other, *terms, *after)


def adam(params, first, second, gradient):
    first = BETA_ONE * first + (1.0 - BETA_ONE) * gradient
    second = BETA_TWO * second + (1.0 - BETA_TWO) * gradient * gradient
    updated = params - LEARN_RATE * (first / (jnp.sqrt(second) + EPSILON) + WEIGHT_DECAY * params)
    return first, second, updated.astype(jnp.bfloat16)


def averaged(own, partner):
    return ((own.astype(jnp.float32) + partner.astype(jnp.float32)) * 0.5).astype(jnp.bfloat16)


def both_steps(distances, x, y, weight, first, second):
    index = lax.axis_index("fsdp")
    core, at_y, at_z = index % CORES, (index // CORES) % Y, index // (Y * CORES)
    bf16, f32 = jnp.bfloat16, jnp.float32
    whole = (0, ROWS)

    def chosen(*pairs):
        rows = [((at_z + dz) % Z_HI) * Y + (at_y + dy) % Y for dy, dz in pairs]
        return jnp.stack(rows).astype(jnp.int32)

    core = core.astype(jnp.int32)[None]
    y_other = core_swap(y)
    pairs = []
    for s in range(2):
        x_own, x_give = turn(core, x, s)
        pairs.append((x_own, core_swap(x_give), y, y_other))

    last = []

    def go(step, chunk, blocks, adds, terms, layout, dtypes):
        outs = products(
            pairs[step], step, chunk, chosen(*blocks), adds, terms, layout, dtypes, tuple(last)
        )
        last[:] = [outs[0]]
        return outs

    def far(step, chunk):
        up, down = go(
            step, chunk, ((2, 0), (2, 1)), ((), ()), (), (((0, *whole),), ((1, *whole),)), (bf16, bf16)
        )
        return y_move(up, 1), y_move(down, -1)

    def near(step, chunk, arrived):
        up, down = go(
            step,
            chunk,
            ((1, 0), (1, 1), (-1, 0), (-1, 1)),
            (((0, 0, *whole),), (), (), ((1, 0, *whole),)),
            arrived,
            (((0, *whole), (1, *whole)), ((2, *whole), (3, *whole))),
            (bf16, bf16),
        )
        return y_move(up, 1), y_move(down, -1)

    def own(step, chunk, arrived):
        mine, give = go(
            step,
            chunk,
            ((0, 0), (0, 1)),
            (((0, 0, *whole), (1, 0, *whole)), ((0, 1, *whole), (1, 1, *whole))),
            arrived,
            (((0, *whole),), ((1, *whole),)),
            (f32, bf16),
        )
        return mine[0] + z_swap(give)[0].astype(f32)

    def across(step, chunk):
        (give,) = go(
            step,
            chunk,
            tuple((dy, 1) for dy in range(Y)),
            ((),) * Y,
            (),
            (tuple((dy, *whole) for dy in range(Y)),),
            (bf16,),
        )
        return z_swap(give)

    def far_across(step, chunk, got):
        up, down = go(
            step,
            chunk,
            ((2, 0),),
            (((0, 2, *whole),),),
            (got,),
            (((0, 0, HALF),), ((0, HALF, ROWS),)),
            (bf16, bf16),
        )
        return y_move(up, 1), y_move(down, -1)

    def near_across(step, chunk, got, arrived):
        up, down = go(
            step,
            chunk,
            ((1, 0), (-1, 0)),
            (((0, 1, *whole), (1, 0, 0, HALF)), ((0, 3, *whole), (2, 0, HALF, ROWS))),
            (got, *arrived),
            (((0, *whole),), ((1, *whole),)),
            (bf16, bf16),
        )
        return y_move(up, 1), y_move(down, -1)

    def own_across(step, chunk, got, arrived):
        (mine,) = go(
            step,
            chunk,
            ((0, 0),),
            (((0, 0, *whole), (1, 0, *whole), (2, 0, *whole)),),
            (got, *arrived),
            (((0, *whole),),),
            (f32,),
        )
        return mine[0]

    def cut(a, chunk):
        return a[:, chunk[0] : chunk[0] + chunk[1]]

    a, b = FIRST
    c, d = SECOND
    far_a = far(0, a)
    got = across(1, LAST)
    far_b = far(0, b)
    near_a = near(0, a, far_a)
    near_b = near(0, b, far_b)
    far_c = far(1, c)
    sum_a = own(0, a, near_a)
    far_d = far(1, d)
    near_c = near(1, c, far_c)
    sum_b = own(0, b, near_b)
    far_last = far_across(1, LAST, got)
    near_d = near(1, d, far_d)
    near_last = near_across(1, LAST, got, far_last)
    sum_c = own(1, c, near_c)
    sum_d = own(1, d, near_d)
    sum_last = own_across(1, LAST, got, near_last)

    state = []
    for chunk, gradient in ((a, sum_a), (b, sum_b)):
        w, m, v = (cut(t[0], chunk).astype(f32) for t in (weight, first, second))
        m, v, u = adam(w, m, v, gradient)
        state.append((m, v, averaged(u, group_move(u, distances[0]))))
    m, v, w = (jnp.concatenate(parts, axis=1) for parts in zip(*state))
    weights, moments = [], []
    for chunk, gradient in ((c, sum_c), (d, sum_d), (LAST, sum_last)):
        m_new, _, u = adam(cut(w, chunk).astype(f32), cut(m, chunk), cut(v, chunk), gradient)
        weights.append(averaged(u, group_move(u, distances[1])))
        moments.append(m_new)
    return jnp.concatenate(weights, axis=1)[None], jnp.concatenate(moments, axis=1)[None]


def per_device(activations, out_grads, weight, first_moment, second_moment, step_index):
    levels = N_GROUP.bit_length() - 1
    branches = [
        partial(both_steps, (1 << level, 1 << ((level + 1) % levels))) for level in range(levels)
    ]
    return lax.switch(
        step_index[0] % levels,
        branches,
        activations,
        out_grads,
        weight,
        first_moment,
        second_moment,
    )


def solution(mesh):
    in_specs = (
        P(None, "group", "fsdp", None),
        P(None, "group", "fsdp", None),
        P("group", "fsdp", None),
        P("group", "fsdp", None),
        P("group", "fsdp", None),
        P(),
    )
    out_specs = (P("group", "fsdp", None), P("group", "fsdp", None))
    return jax.shard_map(
        per_device, mesh=mesh, in_specs=in_specs, out_specs=out_specs, check_vma=False
    )
```

```python
from functools import partial

import jax
import jax.numpy as jnp
from jax import lax
from jax.experimental import pallas as pl
from jax.experimental.pallas import tpu as pltpu
from jax.sharding import PartitionSpec as P

LEARN_RATE = 0.05
WEIGHT_DECAY = 0.1
BETA_ONE = 0.9
BETA_TWO = 0.95
EPSILON = 1e-08

Z_HI, Y, CORES = 2, 4, 2
N_FSDP = Z_HI * Y * CORES
N_GROUP = 16
ROWS = 160
TOK = 384
WIDTH = 2560
FIRST = ((0, 1024), (1024, 1536))
SECOND = ((0, 1024), (1024, 1024))
LAST = (2048, 512)
TILE = 512
HALF = ROWS // 2
STRIP = 16
SMALL = pl.CostEstimate(flops=1024, bytes_accessed=1024, transcendentals=0)
PARAMS = pltpu.CompilerParams(vmem_limit_bytes=28 * 1024 * 1024)


def fsdp_move(block, move):
    def target(i):
        z, y, c = i // (Y * CORES), (i // CORES) % Y, i % CORES
        z, y, c = move(z, y, c)
        return ((z % Z_HI) * Y + y % Y) * CORES + c % CORES

    return lax.ppermute(block, "fsdp", [(i, target(i)) for i in range(N_FSDP)])


def y_move(block, shift):
    return fsdp_move(block, lambda z, y, c: (z, y + shift, c))


def z_swap(block):
    return fsdp_move(block, lambda z, y, c: (z + 1, y, c))


def core_swap(block):
    return fsdp_move(block, lambda z, y, c: (z, y, c + 1))


def group_move(block, distance):
    return lax.ppermute(
        block, "group", [((i - distance) % N_GROUP, i) for i in range(N_GROUP)]
    )


def turn_kernel(core_ref, x_ref, own_ref, other_ref, turned):
    def one(j, carry):
        at = pl.multiple_of(j * 256, 256)
        turned[pl.ds(at, 256), :] = x_ref[:, pl.ds(at, 256)].T
        return carry

    lax.fori_loop(0, WIDTH // 256, one, 0)
    core = core_ref[0]

    def give(b, carry):
        for ref, k in ((own_ref, core), (other_ref, 1 - core)):
            start = pl.multiple_of((b * CORES + k) * ROWS, ROWS)
            ref[b] = turned[pl.ds(start, ROWS), :]
        return carry

    lax.fori_loop(0, Z_HI * Y, give, 0)


def turn(core, x, step):
    shape = jax.ShapeDtypeStruct((Z_HI * Y, ROWS, TOK), jnp.bfloat16)
    return pl.pallas_call(
        turn_kernel,
        grid_spec=pltpu.PrefetchScalarGridSpec(
            num_scalar_prefetch=1,
            grid=(1,),
            in_specs=[pl.BlockSpec((None, None, TOK, WIDTH), lambda i, s: (step, 0, 0, 0))],
            out_specs=[pl.BlockSpec((Z_HI * Y, ROWS, TOK), lambda i, s: (0, 0, 0))] * 2,
            scratch_shapes=[pltpu.VMEM((WIDTH, TOK), jnp.bfloat16)],
        ),
        out_shape=[shape, shape],
        compiler_params=PARAMS,
        cost_estimate=SMALL,
    )(core, x)


def products_kernel(adds, layout, terms, tiles, blocks_ref, *refs):
    units = len(adds)
    own, other = refs[:units], refs[units : 2 * units]
    at = 2 * units + 2 * tiles
    y_own, y_other = refs[2 * units : at - tiles], refs[at - tiles : at]
    given = refs[at : at + terms]
    outs = refs[len(refs) - len(layout) :]
    x = jnp.concatenate(
        [jnp.concatenate([a[0], b[0]], axis=1) for a, b in zip(own, other)], axis=0
    )
    total = jnp.concatenate(
        [
            jnp.dot(
                x,
                jnp.concatenate([a[...], b[...]], axis=0),
                preferred_element_type=jnp.float32,
            )
            for a, b in zip(y_own, y_other)
        ],
        axis=1,
    )
    parts = []
    for u, per_unit in enumerate(adds):
        part = total[u * ROWS : (u + 1) * ROWS]
        for term, plane, low, high in per_unit:
            more = given[term][plane].astype(jnp.float32)
            if (low, high) == (0, ROWS):
                part = part + more
            elif low == 0:
                part = jnp.concatenate([part[:high] + more, part[high:]], axis=0)
            else:
                part = jnp.concatenate([part[:low], part[low:] + more], axis=0)
        parts.append(part)
    for out, planes in zip(outs, layout):
        for p, (u, low, high) in enumerate(planes):
            out[p] = parts[u][low:high].astype(out.dtype)


def products(pair, step, chunk, blocks, adds, terms, layout, dtypes, after=()):
    x_own, x_other, y_own, y_other = pair
    column, width = chunk
    units = len(adds)
    x_specs = [
        pl.BlockSpec((1, ROWS, TOK), lambda j, s, u=u: (s[u], 0, 0)) for u in range(units)
    ]
    tiles = width // TILE
    y_specs = [
        pl.BlockSpec((None, None, TOK, TILE), lambda j, s, t=t: (step, 0, 0, column // TILE + t))
        for t in range(tiles)
    ]

    def piece(planes, rows):
        return pl.BlockSpec((planes, rows, width), lambda j, s: (0, 0, 0))

    outs = [(len(planes), planes[0][2] - planes[0][1], width) for planes in layout]
    return pl.pallas_call(
        partial(products_kernel, adds, layout, len(terms), tiles),
        grid_spec=pltpu.PrefetchScalarGridSpec(
            num_scalar_prefetch=1,
            grid=(1,),
            in_specs=x_specs * 2
            + y_specs * 2
            + [piece(*t.shape[:2]) for t in terms]
            + [pl.BlockSpec(memory_space=pl.ANY)] * len(after),
            out_specs=[piece(*o[:2]) for o in outs],
        ),
        out_shape=[jax.ShapeDtypeStruct(o, d) for o, d in zip(outs, dtypes)],
        compiler_params=PARAMS,
        cost_estimate=SMALL,
    )(blocks, *([x_own] * units), *([x_other] * units), *([y_own] * tiles), *([y_other] * tiles), *terms, *after)


def strips(work):
    def one(i, carry):
        work(pl.ds(pl.multiple_of(i * STRIP, STRIP), STRIP))
        return carry

    lax.fori_loop(0, ROWS // STRIP, one, 0)


def by_columns(kernel, ins, outs, width, after=(), into=None):
    def spec(array, column):
        lead = (None,) * (len(array.shape) - 2)
        return pl.BlockSpec(
            (*lead, ROWS, TILE), lambda j: (*(0 for _ in lead), 0, column // TILE + j)
        )

    shapes = [jax.ShapeDtypeStruct((ROWS, columns), dtype) for columns, _, dtype in outs]
    unread = list(after)
    aliases = {}
    if into is not None:
        aliases = {len(ins) + len(unread): len(outs) - 1}
        unread.append(into)

    def body(*refs):
        used = refs[: len(ins)] + refs[len(ins) + len(unread) :]
        strips(partial(kernel, *used))

    return pl.pallas_call(
        body,
        grid=(width // TILE,),
        in_specs=[spec(*i) for i in ins] + [pl.BlockSpec(memory_space=pl.ANY)] * len(unread),
        out_specs=[spec(shape, o[1]) for shape, o in zip(shapes, outs)],
        out_shape=shapes,
        input_output_aliases=aliases,
        compiler_params=PARAMS,
        cost_estimate=SMALL,
    )(*(i[0] for i in ins), *unread)


def adam(params, first, second, gradient):
    first = BETA_ONE * first + (1.0 - BETA_ONE) * gradient
    second = BETA_TWO * second + (1.0 - BETA_TWO) * gradient * gradient
    updated = params - LEARN_RATE * (first / (jnp.sqrt(second) + EPSILON) + WEIGHT_DECAY * params)
    return first, second, updated.astype(jnp.bfloat16)


def average(own, partner):
    return ((own.astype(jnp.float32) + partner.astype(jnp.float32)) * 0.5).astype(jnp.bfloat16)


def first_kernel(w, m, v, mine, got, new_m, new_v, new_u, at):
    f32 = jnp.float32
    gradient = mine[at] + got[at].astype(f32)
    new_m[at], new_v[at], new_u[at] = adam(
        w[at].astype(f32), m[at].astype(f32), v[at].astype(f32), gradient
    )


def second_kernel(own, partner, m, v, *rest):
    *gradients, new_u, new_m, at = rest
    f32 = jnp.float32
    gradient = gradients[0][at]
    for more in gradients[1:]:
        gradient = gradient + more[at].astype(f32)
    w = average(own[at], partner[at]).astype(f32)
    new_m[at], _, new_u[at] = adam(w, m[at], v[at], gradient)


def average_kernel(own, partner, out, at):
    out[at] = average(own[at], partner[at])


def both_steps(distances, x, y, weight, first, second):
    index = lax.axis_index("fsdp")
    core, at_y, at_z = index % CORES, (index // CORES) % Y, index // (Y * CORES)
    bf16, f32 = jnp.bfloat16, jnp.float32
    whole = (0, ROWS)

    def chosen(*pairs):
        rows = [((at_z + dz) % Z_HI) * Y + (at_y + dy) % Y for dy, dz in pairs]
        return jnp.stack(rows).astype(jnp.int32)

    core = core.astype(jnp.int32)[None]
    y_other = core_swap(y)
    pairs = []
    for s in range(2):
        x_own, x_give = turn(core, x, s)
        pairs.append((x_own, core_swap(x_give), y, y_other))

    last = []

    def go(step, chunk, blocks, adds, terms, layout, dtypes):
        outs = products(
            pairs[step], step, chunk, chosen(*blocks), adds, terms, layout, dtypes, tuple(last)
        )
        last[:] = [outs[0]]
        return outs

    def far(step, chunk):
        up, down = go(
            step, chunk, ((2, 0), (2, 1)), ((), ()), (), (((0, *whole),), ((1, *whole),)), (bf16, bf16)
        )
        return y_move(up, 1), y_move(down, -1)

    def near(step, chunk, arrived):
        up, down = go(
            step,
            chunk,
            ((1, 0), (1, 1), (-1, 0), (-1, 1)),
            (((0, 0, *whole),), (), (), ((1, 0, *whole),)),
            arrived,
            (((0, *whole), (1, *whole)), ((2, *whole), (3, *whole))),
            (bf16, bf16),
        )
        return y_move(up, 1), y_move(down, -1)

    def own(step, chunk, arrived):
        mine, give = go(
            step,
            chunk,
            ((0, 0), (0, 1)),
            (((0, 0, *whole), (1, 0, *whole)), ((0, 1, *whole), (1, 1, *whole))),
            arrived,
            (((0, *whole),), ((1, *whole),)),
            (f32, bf16),
        )
        return mine, z_swap(give)

    def across(step, chunk):
        (give,) = go(
            step,
            chunk,
            tuple((dy, 1) for dy in range(Y)),
            ((),) * Y,
            (),
            (tuple((dy, *whole) for dy in range(Y)),),
            (bf16,),
        )
        return z_swap(give)

    def far_across(step, chunk, got):
        up, down = go(
            step,
            chunk,
            ((2, 0),),
            (((0, 2, *whole),),),
            (got,),
            (((0, 0, HALF),), ((0, HALF, ROWS),)),
            (bf16, bf16),
        )
        return y_move(up, 1), y_move(down, -1)

    def near_across(step, chunk, got, arrived):
        up, down = go(
            step,
            chunk,
            ((1, 0), (-1, 0)),
            (((0, 1, *whole), (1, 0, 0, HALF)), ((0, 3, *whole), (2, 0, HALF, ROWS))),
            (got, *arrived),
            (((0, *whole),), ((1, *whole),)),
            (bf16, bf16),
        )
        return y_move(up, 1), y_move(down, -1)

    def own_across(step, chunk, got, arrived):
        (mine,) = go(
            step,
            chunk,
            ((0, 0),),
            (((0, 0, *whole), (1, 0, *whole), (2, 0, *whole)),),
            (got, *arrived),
            (((0, *whole),),),
            (f32,),
        )
        return (mine,)

    def follow(kernel, ins, outs, width, into=None):
        results = by_columns(kernel, ins, outs, width, tuple(last), into)
        last[:] = [results[0]]
        return results

    def first_step(chunk, sums):
        column, width = chunk
        m, v, u = follow(
            first_kernel,
            [(weight, column), (first, column), (second, column)] + [(t, 0) for t in sums],
            [(width, 0, f32), (width, 0, f32), (width, 0, bf16)],
            width,
        )
        return u, group_move(u, distances[0]), m, v

    def second_step(chunk, offset, state, sums, moments):
        column, width = chunk
        u, moments = follow(
            second_kernel,
            [(t, offset) for t in state] + [(t, 0) for t in sums],
            [(width, 0, bf16), (WIDTH, column, f32)],
            width,
            moments,
        )
        return (u, group_move(u, distances[1])), moments

    def finish(chunk, both, weights):
        column, width = chunk
        (weights,) = follow(
            average_kernel, [(t, 0) for t in both], [(WIDTH, column, bf16)], width, weights
        )
        return weights

    a, b = FIRST
    c, d = SECOND
    far_a = far(0, a)
    far_b = far(0, b)
    got = across(1, LAST)
    near_a = near(0, a, far_a)
    near_b = near(0, b, far_b)
    far_c = far(1, c)
    far_d = far(1, d)
    sums_a = own(0, a, near_a)
    far_last = far_across(1, LAST, got)
    sums_b = own(0, b, near_b)
    near_c = near(1, c, far_c)
    state_a = first_step(a, sums_a)
    near_d = near(1, d, far_d)
    near_last = near_across(1, LAST, got, far_last)
    state_b = first_step(b, sums_b)
    sums_c = own(1, c, near_c)
    sums_d = own(1, d, near_d)
    sums_last = own_across(1, LAST, got, near_last)
    both_c, moments = second_step(c, 0, state_a, sums_c, None)
    both_last, moments = second_step(LAST, LAST[0] - b[0], state_b, sums_last, moments)
    both_d, moments = second_step(d, 0, state_b, sums_d, moments)
    weights = finish(c, both_c, None)
    weights = finish(LAST, both_last, weights)
    weights = finish(d, both_d, weights)
    return weights[None], moments[None]


def per_device(activations, out_grads, weight, first_moment, second_moment, step_index):
    levels = N_GROUP.bit_length() - 1
    branches = [
        partial(both_steps, (1 << level, 1 << ((level + 1) % levels))) for level in range(levels)
    ]
    return lax.switch(
        step_index[0] % levels,
        branches,
        activations,
        out_grads,
        weight,
        first_moment,
        second_moment,
    )


def solution(mesh):
    in_specs = (
        P(None, "group", "fsdp", None),
        P(None, "group", "fsdp", None),
        P("group", "fsdp", None),
        P("group", "fsdp", None),
        P("group", "fsdp", None),
        P(),
    )
    out_specs = (P("group", "fsdp", None), P("group", "fsdp", None))
    return jax.shard_map(
        per_device, mesh=mesh, in_specs=in_specs, out_specs=out_specs, check_vma=False
    )
```

```python
from functools import partial

import jax
import jax.numpy as jnp
from jax import lax
from jax.experimental import pallas as pl
from jax.experimental.pallas import tpu as pltpu
from jax.sharding import PartitionSpec as P

LEARN_RATE = 0.05
WEIGHT_DECAY = 0.1
BETA_ONE = 0.9
BETA_TWO = 0.95
EPSILON = 1e-08

Z_HI, Y, CORES = 2, 4, 2
N_FSDP = Z_HI * Y * CORES
N_GROUP = 16
ROWS = 160
TOK = 384
WIDTH = 2560
FIRST = ((0, 1024), (1024, 1536))
SECOND = ((0, 1024), (1024, 1024))
LAST = (2048, 512)
TILE = 512
HALF = ROWS // 2
STRIP = 16
SMALL = pl.CostEstimate(flops=1024, bytes_accessed=1024, transcendentals=0)
PARAMS = pltpu.CompilerParams(vmem_limit_bytes=28 * 1024 * 1024)


def fsdp_move(block, move):
    def target(i):
        z, y, c = i // (Y * CORES), (i // CORES) % Y, i % CORES
        z, y, c = move(z, y, c)
        return ((z % Z_HI) * Y + y % Y) * CORES + c % CORES

    return lax.ppermute(block, "fsdp", [(i, target(i)) for i in range(N_FSDP)])


def y_move(block, shift):
    return fsdp_move(block, lambda z, y, c: (z, y + shift, c))


def y_sum(blocks):
    groups = [
        [(z * Y + y) * CORES + c for y in range(Y)] for z in range(Z_HI) for c in range(CORES)
    ]
    return lax.psum_scatter(
        blocks, "fsdp", scatter_dimension=0, axis_index_groups=groups, tiled=True
    )


def z_swap(block):
    return fsdp_move(block, lambda z, y, c: (z + 1, y, c))


def core_swap(block):
    return fsdp_move(block, lambda z, y, c: (z, y, c + 1))


def group_move(block, distance):
    return lax.ppermute(
        block, "group", [((i - distance) % N_GROUP, i) for i in range(N_GROUP)]
    )


def turn_kernel(core_ref, x_ref, own_ref, other_ref, turned):
    def one(j, carry):
        at = pl.multiple_of(j * 256, 256)
        turned[pl.ds(at, 256), :] = x_ref[:, pl.ds(at, 256)].T
        return carry

    lax.fori_loop(0, WIDTH // 256, one, 0)
    core = core_ref[0]

    def give(b, carry):
        for ref, k in ((own_ref, core), (other_ref, 1 - core)):
            start = pl.multiple_of((b * CORES + k) * ROWS, ROWS)
            ref[b] = turned[pl.ds(start, ROWS), :]
        return carry

    lax.fori_loop(0, Z_HI * Y, give, 0)


def turn(core, x, step):
    shape = jax.ShapeDtypeStruct((Z_HI * Y, ROWS, TOK), jnp.bfloat16)
    return pl.pallas_call(
        turn_kernel,
        grid_spec=pltpu.PrefetchScalarGridSpec(
            num_scalar_prefetch=1,
            grid=(1,),
            in_specs=[pl.BlockSpec((None, None, TOK, WIDTH), lambda i, s: (step, 0, 0, 0))],
            out_specs=[pl.BlockSpec((Z_HI * Y, ROWS, TOK), lambda i, s: (0, 0, 0))] * 2,
            scratch_shapes=[pltpu.VMEM((WIDTH, TOK), jnp.bfloat16)],
        ),
        out_shape=[shape, shape],
        compiler_params=PARAMS,
        cost_estimate=SMALL,
    )(core, x)


def products_kernel(adds, layout, terms, tiles, blocks_ref, *refs):
    units = len(adds)
    own, other = refs[:units], refs[units : 2 * units]
    at = 2 * units + 2 * tiles
    y_own, y_other = refs[2 * units : at - tiles], refs[at - tiles : at]
    given = refs[at : at + terms]
    outs = refs[len(refs) - len(layout) :]
    x = jnp.concatenate(
        [jnp.concatenate([a[0], b[0]], axis=1) for a, b in zip(own, other)], axis=0
    )
    total = jnp.concatenate(
        [
            jnp.dot(
                x,
                jnp.concatenate([a[...], b[...]], axis=0),
                preferred_element_type=jnp.float32,
            )
            for a, b in zip(y_own, y_other)
        ],
        axis=1,
    )
    parts = []
    for u, per_unit in enumerate(adds):
        part = total[u * ROWS : (u + 1) * ROWS]
        for term, plane, low, high in per_unit:
            more = given[term][plane].astype(jnp.float32)
            if (low, high) == (0, ROWS):
                part = part + more
            elif low == 0:
                part = jnp.concatenate([part[:high] + more, part[high:]], axis=0)
            else:
                part = jnp.concatenate([part[:low], part[low:] + more], axis=0)
        parts.append(part)
    for out, planes in zip(outs, layout):
        for p, (u, low, high) in enumerate(planes):
            out[p] = parts[u][low:high].astype(out.dtype)


def products(pair, step, chunk, blocks, adds, terms, layout, dtypes, after=()):
    x_own, x_other, y_own, y_other = pair
    column, width = chunk
    units = len(adds)
    x_specs = [
        pl.BlockSpec((1, ROWS, TOK), lambda j, s, u=u: (s[u], 0, 0)) for u in range(units)
    ]
    tiles = width // TILE
    y_specs = [
        pl.BlockSpec((None, None, TOK, TILE), lambda j, s, t=t: (step, 0, 0, column // TILE + t))
        for t in range(tiles)
    ]

    def piece(planes, rows):
        return pl.BlockSpec((planes, rows, width), lambda j, s: (0, 0, 0))

    outs = [(len(planes), planes[0][2] - planes[0][1], width) for planes in layout]
    return pl.pallas_call(
        partial(products_kernel, adds, layout, len(terms), tiles),
        grid_spec=pltpu.PrefetchScalarGridSpec(
            num_scalar_prefetch=1,
            grid=(1,),
            in_specs=x_specs * 2
            + y_specs * 2
            + [piece(*t.shape[:2]) for t in terms]
            + [pl.BlockSpec(memory_space=pl.ANY)] * len(after),
            out_specs=[piece(*o[:2]) for o in outs],
        ),
        out_shape=[jax.ShapeDtypeStruct(o, d) for o, d in zip(outs, dtypes)],
        compiler_params=PARAMS,
        cost_estimate=SMALL,
    )(blocks, *([x_own] * units), *([x_other] * units), *([y_own] * tiles), *([y_other] * tiles), *terms, *after)


def strips(work):
    def one(i, carry):
        work(pl.ds(pl.multiple_of(i * STRIP, STRIP), STRIP))
        return carry

    lax.fori_loop(0, ROWS // STRIP, one, 0)


def by_columns(kernel, ins, outs, width, after=(), into=None):
    def spec(array, column):
        lead = (None,) * (len(array.shape) - 2)
        return pl.BlockSpec(
            (*lead, ROWS, TILE), lambda j: (*(0 for _ in lead), 0, column // TILE + j)
        )

    shapes = [jax.ShapeDtypeStruct((ROWS, columns), dtype) for columns, _, dtype in outs]
    unread = list(after)
    aliases = {}
    if into is not None:
        aliases = {len(ins) + len(unread): len(outs) - 1}
        unread.append(into)

    def body(*refs):
        used = refs[: len(ins)] + refs[len(ins) + len(unread) :]
        strips(partial(kernel, *used))

    return pl.pallas_call(
        body,
        grid=(width // TILE,),
        in_specs=[spec(*i) for i in ins] + [pl.BlockSpec(memory_space=pl.ANY)] * len(unread),
        out_specs=[spec(shape, o[1]) for shape, o in zip(shapes, outs)],
        out_shape=shapes,
        input_output_aliases=aliases,
        compiler_params=PARAMS,
        cost_estimate=SMALL,
    )(*(i[0] for i in ins), *unread)


def adam(params, first, second, gradient):
    first = BETA_ONE * first + (1.0 - BETA_ONE) * gradient
    second = BETA_TWO * second + (1.0 - BETA_TWO) * gradient * gradient
    updated = params - LEARN_RATE * (first / (jnp.sqrt(second) + EPSILON) + WEIGHT_DECAY * params)
    return first, second, updated.astype(jnp.bfloat16)


def average(own, partner):
    return ((own.astype(jnp.float32) + partner.astype(jnp.float32)) * 0.5).astype(jnp.bfloat16)


def first_kernel(w, m, v, mine, got, new_m, new_v, new_u, at):
    f32 = jnp.float32
    gradient = mine[at] + got[at].astype(f32)
    new_m[at], new_v[at], new_u[at] = adam(
        w[at].astype(f32), m[at].astype(f32), v[at].astype(f32), gradient
    )


def second_kernel(own, partner, m, v, *rest):
    *gradients, new_u, new_m, at = rest
    f32 = jnp.float32
    gradient = gradients[0][at].astype(f32)
    for more in gradients[1:]:
        gradient = gradient + more[at].astype(f32)
    w = average(own[at], partner[at]).astype(f32)
    new_m[at], _, new_u[at] = adam(w, m[at], v[at], gradient)


def split_kernel(both, _, mine, give):
    def one(at):
        mine[0, at] = both[0, at]
        give[0, at] = both[1, at]

    strips(one)


def average_kernel(own, partner, out, at):
    out[at] = average(own[at], partner[at])


def both_steps(distances, x, y, weight, first, second):
    index = lax.axis_index("fsdp")
    core, at_y, at_z = index % CORES, (index // CORES) % Y, index // (Y * CORES)
    bf16, f32 = jnp.bfloat16, jnp.float32
    whole = (0, ROWS)

    def chosen(*pairs):
        rows = [((at_z + dz) % Z_HI) * Y + (at_y + dy) % Y for dy, dz in pairs]
        return jnp.stack(rows).astype(jnp.int32)

    core = core.astype(jnp.int32)[None]
    y_other = core_swap(y)
    pairs = []
    for s in range(2):
        x_own, x_give = turn(core, x, s)
        pairs.append((x_own, core_swap(x_give), y, y_other))

    last = []

    def go(step, chunk, blocks, adds, terms, layout, dtypes):
        outs = products(
            pairs[step], step, chunk, chosen(*blocks), adds, terms, layout, dtypes, tuple(last)
        )
        last[:] = [outs[0]]
        return outs

    def far(step, chunk):
        up, down = go(
            step, chunk, ((2, 0), (2, 1)), ((), ()), (), (((0, *whole),), ((1, *whole),)), (bf16, bf16)
        )
        return y_move(up, 1), y_move(down, -1)

    def near(step, chunk, arrived):
        up, down = go(
            step,
            chunk,
            ((1, 0), (1, 1), (-1, 0), (-1, 1)),
            (((0, 0, *whole),), (), (), ((1, 0, *whole),)),
            arrived,
            (((0, *whole), (1, *whole)), ((2, *whole), (3, *whole))),
            (bf16, bf16),
        )
        return y_move(up, 1), y_move(down, -1)

    def own(step, chunk, arrived):
        mine, give = go(
            step,
            chunk,
            ((0, 0), (0, 1)),
            (((0, 0, *whole), (1, 0, *whole)), ((0, 1, *whole), (1, 1, *whole))),
            arrived,
            (((0, *whole),), ((1, *whole),)),
            (f32, bf16),
        )
        return mine, z_swap(give)

    def across(step, chunk):
        (give,) = go(
            step,
            chunk,
            tuple((y - at_y, 1) for y in range(Y)),
            ((),) * Y,
            (),
            (tuple((dy, *whole) for dy in range(Y)),),
            (bf16,),
        )
        return z_swap(give)

    def summed(step, chunk, planes, got):
        units = tuple((y - at_y, dz) for y in range(Y) for dz in range(planes))
        (parts,) = go(
            step,
            chunk,
            units,
            tuple(((t, u, *whole),) for t in range(len(got)) for u in range(Y)) or ((),) * len(units),
            got,
            (tuple((u, *whole) for u in range(len(units))),),
            (bf16,),
        )
        return y_sum(parts)

    def follow(kernel, ins, outs, width, into=None):
        results = by_columns(kernel, ins, outs, width, tuple(last), into)
        last[:] = [results[0]]
        return results

    def first_step(chunk, sums):
        column, width = chunk
        m, v, u = follow(
            first_kernel,
            [(weight, column), (first, column), (second, column)] + [(t, 0) for t in sums],
            [(width, 0, f32), (width, 0, f32), (width, 0, bf16)],
            width,
        )
        return u, group_move(u, distances[0]), m, v

    def second_step(chunk, offset, state, sums, moments):
        column, width = chunk
        u, moments = follow(
            second_kernel,
            [(t, offset) for t in state] + [(t, 0) for t in sums],
            [(width, 0, bf16), (WIDTH, column, f32)],
            width,
            moments,
        )
        return (u, group_move(u, distances[1])), moments

    def finish(chunk, both, weights):
        column, width = chunk
        (weights,) = follow(
            average_kernel, [(t, 0) for t in both], [(WIDTH, column, bf16)], width, weights
        )
        return weights

    def split(chunk, both):
        width = chunk[1]
        mine, give = pl.pallas_call(
            split_kernel,
            in_specs=[
                pl.BlockSpec(memory_space=pltpu.VMEM),
                pl.BlockSpec(memory_space=pl.ANY),
            ],
            out_specs=[pl.BlockSpec(memory_space=pltpu.VMEM)] * 2,
            out_shape=[jax.ShapeDtypeStruct((1, ROWS, width), bf16)] * 2,
            compiler_params=PARAMS,
            cost_estimate=SMALL,
        )(both, *last)
        last[:] = [mine]
        return mine, z_swap(give)

    a, b = FIRST
    c, d = SECOND
    far_a = far(0, a)
    sum_c = summed(1, c, Z_HI, ())
    far_b = far(0, b)
    got = across(1, LAST)
    near_a = near(0, a, far_a)
    near_b = near(0, b, far_b)
    sum_d = summed(1, d, Z_HI, ())
    sums_a = own(0, a, near_a)
    sum_last = summed(1, LAST, 1, (got,))
    sums_b = own(0, b, near_b)
    state_a = first_step(a, sums_a)
    sums_c = split(c, sum_c)
    state_b = first_step(b, sums_b)
    sums_d = split(d, sum_d)
    both_c, moments = second_step(c, 0, state_a, sums_c, None)
    both_last, moments = second_step(LAST, LAST[0] - b[0], state_b, (sum_last,), moments)
    both_d, moments = second_step(d, 0, state_b, sums_d, moments)
    weights = finish(c, both_c, None)
    weights = finish(LAST, both_last, weights)
    weights = finish(d, both_d, weights)
    return weights[None], moments[None]


def per_device(activations, out_grads, weight, first_moment, second_moment, step_index):
    levels = N_GROUP.bit_length() - 1
    branches = [
        partial(both_steps, (1 << level, 1 << ((level + 1) % levels))) for level in range(levels)
    ]
    return lax.switch(
        step_index[0] % levels,
        branches,
        activations,
        out_grads,
        weight,
        first_moment,
        second_moment,
    )


def solution(mesh):
    in_specs = (
        P(None, "group", "fsdp", None),
        P(None, "group", "fsdp", None),
        P("group", "fsdp", None),
        P("group", "fsdp", None),
        P("group", "fsdp", None),
        P(),
    )
    out_specs = (P("group", "fsdp", None), P("group", "fsdp", None))
    return jax.shard_map(
        per_device, mesh=mesh, in_specs=in_specs, out_specs=out_specs, check_vma=False
    )
```

```python
from functools import partial

import jax
import jax.numpy as jnp
from jax import lax
from jax.experimental import pallas as pl
from jax.experimental.pallas import tpu as pltpu
from jax.sharding import PartitionSpec as P

LEARN_RATE = 0.05
WEIGHT_DECAY = 0.1
BETA_ONE = 0.9
BETA_TWO = 0.95
EPSILON = 1e-08

Z_HI, Y, CORES = 2, 4, 2
N_FSDP = Z_HI * Y * CORES
N_GROUP = 16
ROWS = 160
TOK = 384
WIDTH = 2560
CHUNKS = ((0, 1280), (1280, 1280))
TILE = 1280
STRIP = 16
SMALL = pl.CostEstimate(flops=1024, bytes_accessed=1024, transcendentals=0)
PARAMS = pltpu.CompilerParams(vmem_limit_bytes=32 * 1024 * 1024)


def fsdp_move(block, move):
    def target(i):
        z, y, c = i // (Y * CORES), (i // CORES) % Y, i % CORES
        z, y, c = move(z, y, c)
        return ((z % Z_HI) * Y + y % Y) * CORES + c % CORES

    return lax.ppermute(block, "fsdp", [(i, target(i)) for i in range(N_FSDP)])


def y_move(block, shift):
    return fsdp_move(block, lambda z, y, c: (z, y + shift, c))


def z_swap(block):
    return fsdp_move(block, lambda z, y, c: (z + 1, y, c))


def core_swap(block):
    return fsdp_move(block, lambda z, y, c: (z, y, c + 1))


def group_move(block, distance):
    return lax.ppermute(
        block, "group", [((i - distance) % N_GROUP, i) for i in range(N_GROUP)]
    )


def turn_kernel(core_ref, x_ref, *refs):
    own_ref, other_ref, turned = refs[-3:]

    def one(j, carry):
        at = pl.multiple_of(j * 256, 256)
        turned[pl.ds(at, 256), :] = x_ref[:, pl.ds(at, 256)].T
        return carry

    lax.fori_loop(0, WIDTH // 256, one, 0)
    core = core_ref[0]

    def give(b, carry):
        for ref, k in ((own_ref, core), (other_ref, 1 - core)):
            start = pl.multiple_of((b * CORES + k) * ROWS, ROWS)
            ref[b] = turned[pl.ds(start, ROWS), :]
        return carry

    lax.fori_loop(0, Z_HI * Y, give, 0)


def turn(core, x, step, after):
    shape = jax.ShapeDtypeStruct((Z_HI * Y, ROWS, TOK), jnp.bfloat16)
    return pl.pallas_call(
        turn_kernel,
        grid_spec=pltpu.PrefetchScalarGridSpec(
            num_scalar_prefetch=1,
            grid=(1,),
            in_specs=[pl.BlockSpec((None, None, TOK, WIDTH), lambda i, s: (step, 0, 0, 0))]
            + [pl.BlockSpec(memory_space=pl.ANY)] * len(after),
            out_specs=[pl.BlockSpec((Z_HI * Y, ROWS, TOK), lambda i, s: (0, 0, 0))] * 2,
            scratch_shapes=[pltpu.VMEM((WIDTH, TOK), jnp.bfloat16)],
        ),
        out_shape=[shape, shape],
        compiler_params=PARAMS,
        cost_estimate=SMALL,
    )(core, x, *after)


def products_kernel(adds, layout, terms, tiles, blocks_ref, *refs):
    units = len(adds)
    own, other = refs[:units], refs[units : 2 * units]
    at = 2 * units + 2 * tiles
    y_own, y_other = refs[2 * units : at - tiles], refs[at - tiles : at]
    given = [refs[at + t * tiles : at + (t + 1) * tiles] for t in range(terms)]
    outs = refs[len(refs) - len(layout) :]
    x = jnp.concatenate(
        [jnp.concatenate([a[0], b[0]], axis=1) for a, b in zip(own, other)], axis=0
    )
    total = jnp.concatenate(
        [
            jnp.dot(
                x,
                jnp.concatenate([a[...], b[...]], axis=0),
                preferred_element_type=jnp.float32,
            )
            for a, b in zip(y_own, y_other)
        ],
        axis=1,
    )
    parts = []
    for u, per_unit in enumerate(adds):
        part = total[u * ROWS : (u + 1) * ROWS]
        for term, plane in per_unit:
            more = jnp.concatenate([r[plane] for r in given[term]], axis=1)
            part = part + more.astype(jnp.float32)
        parts.append(part)
    for out, planes in zip(outs, layout):
        for p, u in enumerate(planes):
            out[p] = parts[u].astype(out.dtype)


def products(pair, step, chunk, blocks, adds, terms, layout, dtypes, after=()):
    x_own, x_other, y_own, y_other = pair
    column, width = chunk
    units = len(adds)
    x_specs = [
        pl.BlockSpec((1, ROWS, TOK), lambda j, s, u=u: (s[u], 0, 0)) for u in range(units)
    ]
    tiles = width // TILE
    y_specs = [
        pl.BlockSpec((None, None, TOK, TILE), lambda j, s, t=t: (step, 0, 0, column // TILE + t))
        for t in range(tiles)
    ]

    t_specs = [
        pl.BlockSpec((t.shape[0], ROWS, TILE), lambda j, s, k=first // TILE + k: (0, 0, k))
        for t, first in terms
        for k in range(tiles)
    ]
    outs = [(len(planes), ROWS, width) for planes in layout]
    return pl.pallas_call(
        partial(products_kernel, adds, layout, len(terms), tiles),
        grid_spec=pltpu.PrefetchScalarGridSpec(
            num_scalar_prefetch=1,
            grid=(1,),
            in_specs=x_specs * 2
            + y_specs * 2
            + t_specs
            + [pl.BlockSpec(memory_space=pl.ANY)] * len(after),
            out_specs=[pl.BlockSpec(o, lambda j, s: (0, 0, 0)) for o in outs],
        ),
        out_shape=[jax.ShapeDtypeStruct(o, d) for o, d in zip(outs, dtypes)],
        compiler_params=PARAMS,
        cost_estimate=SMALL,
    )(blocks, *([x_own] * units), *([x_other] * units), *([y_own] * tiles), *([y_other] * tiles), *(t for t, _ in terms for _ in range(tiles)), *after)


def strips(work):
    def one(i, carry):
        work(pl.ds(pl.multiple_of(i * STRIP, STRIP), STRIP))
        return carry

    lax.fori_loop(0, ROWS // STRIP, one, 0)


def by_columns(kernel, ins, outs, width, after=(), into=None):
    def spec(array, column, plane=0):
        lead = (None,) * (len(array.shape) - 2)
        return pl.BlockSpec(
            (*lead, ROWS, TILE), lambda j: (*(plane for _ in lead), 0, column // TILE + j)
        )

    shapes = [jax.ShapeDtypeStruct((ROWS, columns), dtype) for columns, _, dtype in outs]
    unread = list(after)
    aliases = {}
    if into is not None:
        aliases = {len(ins) + len(unread): len(outs) - 1}
        unread.append(into)

    def body(*refs):
        used = refs[: len(ins)] + refs[len(ins) + len(unread) :]
        strips(partial(kernel, *used))

    return pl.pallas_call(
        body,
        grid=(width // TILE,),
        in_specs=[spec(*i) for i in ins] + [pl.BlockSpec(memory_space=pl.ANY)] * len(unread),
        out_specs=[spec(shape, o[1]) for shape, o in zip(shapes, outs)],
        out_shape=shapes,
        input_output_aliases=aliases,
        compiler_params=PARAMS,
        cost_estimate=SMALL,
    )(*(i[0] for i in ins), *unread)


def adam(params, first, second, gradient):
    first = BETA_ONE * first + (1.0 - BETA_ONE) * gradient
    second = BETA_TWO * second + (1.0 - BETA_TWO) * gradient * gradient
    updated = params - LEARN_RATE * (first / (jnp.sqrt(second) + EPSILON) + WEIGHT_DECAY * params)
    return first, second, updated.astype(jnp.bfloat16)


def average(own, partner):
    return ((own.astype(jnp.float32) + partner.astype(jnp.float32)) * 0.5).astype(jnp.bfloat16)


def gradient_of(terms, at):
    total = terms[0][at].astype(jnp.float32)
    for term in terms[1:]:
        total = total + term[at].astype(jnp.float32)
    return total


def first_kernel(w, m, v, *rest):
    *terms, new_m, new_v, new_u, at = rest
    f32 = jnp.float32
    new_m[at], new_v[at], new_u[at] = adam(
        w[at].astype(f32), m[at].astype(f32), v[at].astype(f32), gradient_of(terms, at)
    )


def second_kernel(own, partner, m, v, *rest):
    *terms, new_u, new_m, at = rest
    w = average(own[at], partner[at]).astype(jnp.float32)
    new_m[at], _, new_u[at] = adam(w, m[at], v[at], gradient_of(terms, at))


def give_kernel(own, up, down, out, at):
    out[at] = gradient_of((own, up, down), at).astype(out.dtype)


def average_kernel(own, partner, out, at):
    out[at] = average(own[at], partner[at])


def both_steps(distances, x, y, weight, first, second):
    index = lax.axis_index("fsdp")
    core, at_y, at_z = index % CORES, (index // CORES) % Y, index // (Y * CORES)
    bf16, f32 = jnp.bfloat16, jnp.float32

    def chosen(*pairs):
        rows = [((at_z + dz) % Z_HI) * Y + (at_y + dy) % Y for dy, dz in pairs]
        return jnp.stack(rows).astype(jnp.int32)

    core = core.astype(jnp.int32)[None]
    y_other = core_swap(y)
    last = []
    pairs = []
    for s in range(2):
        x_own, x_give = turn(core, x, s, tuple(last))
        last[:] = [x_own]
        pairs.append((x_own, core_swap(x_give), y, y_other))

    def go(step, chunk, blocks, adds, terms, layout, after=()):
        outs = products(
            pairs[step],
            step,
            chunk,
            chosen(*blocks),
            adds,
            terms,
            layout,
            (bf16,) * len(layout),
            (*last, *after),
        )
        last[:] = [outs[0]]
        return outs

    def far(step, chunk):
        up, down = go(step, chunk, ((2, 0), (2, 1)), ((), ()), (), ((0,), (1,)))
        return y_move(up, 1), y_move(down, -1)

    def near(step, chunk, arrived, after=()):
        up, down, mine, other = go(
            step,
            chunk,
            ((1, 0), (1, 1), (-1, 0), (-1, 1), (0, 0), (0, 1)),
            (((0, 0),), (), (), ((1, 0),), (), ()),
            [(t, chunk[0]) for t in arrived],
            ((0, 1), (2, 3), (4,), (5,)),
            after,
        )
        return y_move(up, 1), y_move(down, -1), mine, other

    def follow(kernel, ins, outs, width, into=None):
        results = by_columns(kernel, ins, outs, width, tuple(last), into)
        last[:] = [results[0]]
        return results

    def across(chunk, sums):
        up, down, mine, other = sums
        (give,) = follow(
            give_kernel,
            [(other, 0), (up, 0, 1), (down, 0, 1)],
            [(chunk[1], 0, bf16)],
            chunk[1],
        )
        return [(mine, 0), (up, 0), (down, 0), (z_swap(give), 0)]

    def first_step(chunk, terms):
        column, width = chunk
        m, v, u = follow(
            first_kernel,
            [(weight, column), (first, column), (second, column)] + terms,
            [(width, 0, f32), (width, 0, f32), (width, 0, bf16)],
            width,
        )
        return u, group_move(u, distances[0]), m, v

    def second_step(chunk, state, terms, moments):
        column, width = chunk
        u, moments = follow(
            second_kernel,
            [(t, 0) for t in state] + terms,
            [(width, 0, bf16), (WIDTH, column, f32)],
            width,
            moments,
        )
        return (u, group_move(u, distances[1])), moments

    def finish(chunk, both, weights):
        column, width = chunk
        (weights,) = follow(
            average_kernel, [(t, 0) for t in both], [(WIDTH, column, bf16)], width, weights
        )
        return weights

    a, b = CHUNKS
    far_ab = far(0, (0, WIDTH))
    far_cd = far(1, (0, WIDTH))
    near_a = near(0, a, far_ab)
    near_b = near(0, b, far_ab, far_cd)
    terms_a = across(a, near_a)
    near_c = near(1, a, far_cd)
    terms_b = across(b, near_b)
    near_d = near(1, b, far_cd)
    state_a = first_step(a, terms_a)
    terms_c = across(a, near_c)
    state_b = first_step(b, terms_b)
    terms_d = across(b, near_d)
    both_c, moments = second_step(a, state_a, terms_c, None)
    both_d, moments = second_step(b, state_b, terms_d, moments)
    weights = finish(a, both_c, None)
    weights = finish(b, both_d, weights)
    return weights[None], moments[None]


def per_device(activations, out_grads, weight, first_moment, second_moment, step_index):
    levels = N_GROUP.bit_length() - 1
    branches = [
        partial(both_steps, (1 << level, 1 << ((level + 1) % levels))) for level in range(levels)
    ]
    return lax.switch(
        step_index[0] % levels,
        branches,
        activations,
        out_grads,
        weight,
        first_moment,
        second_moment,
    )


def solution(mesh):
    in_specs = (
        P(None, "group", "fsdp", None),
        P(None, "group", "fsdp", None),
        P("group", "fsdp", None),
        P("group", "fsdp", None),
        P("group", "fsdp", None),
        P(),
    )
    out_specs = (P("group", "fsdp", None), P("group", "fsdp", None))
    return jax.shard_map(
        per_device, mesh=mesh, in_specs=in_specs, out_specs=out_specs, check_vma=False
    )
```

```python
from functools import partial

import jax
import jax.numpy as jnp
from jax import lax
from jax.experimental import pallas as pl
from jax.experimental.pallas import tpu as pltpu
from jax.sharding import PartitionSpec as P

LEARN_RATE = 0.05
WEIGHT_DECAY = 0.1
BETA_ONE = 0.9
BETA_TWO = 0.95
EPSILON = 1e-08

Z_HI, Y, CORES = 2, 4, 2
N_FSDP = Z_HI * Y * CORES
N_GROUP = 16
LEVELS = N_GROUP.bit_length() - 1
ROWS = 160
TOK = 384
WIDTH = 2560
CHUNKS = ((0, 1280), (1280, 1280))
TILE = 1280
STRIP = 16
SMALL = pl.CostEstimate(flops=1024, bytes_accessed=1024, transcendentals=0)
PARAMS = pltpu.CompilerParams(vmem_limit_bytes=32 * 1024 * 1024)


def fsdp_move(block, move):
    def target(i):
        z, y, c = i // (Y * CORES), (i // CORES) % Y, i % CORES
        z, y, c = move(z, y, c)
        return ((z % Z_HI) * Y + y % Y) * CORES + c % CORES

    return lax.ppermute(block, "fsdp", [(i, target(i)) for i in range(N_FSDP)])


def y_move(block, shift):
    return fsdp_move(block, lambda z, y, c: (z, y + shift, c))


def z_swap(block):
    return fsdp_move(block, lambda z, y, c: (z + 1, y, c))


def core_swap(block):
    return fsdp_move(block, lambda z, y, c: (z, y, c + 1))


def group_move(level, block):
    def moved(distance, block):
        return lax.ppermute(
            block, "group", [((i - distance) % N_GROUP, i) for i in range(N_GROUP)]
        )

    return lax.switch(level, [partial(moved, 1 << k) for k in range(LEVELS)], block)


def turn_kernel(core_ref, x_ref, *refs):
    own_ref, other_ref, turned = refs[-3:]

    def one(j, carry):
        at = pl.multiple_of(j * 256, 256)
        turned[pl.ds(at, 256), :] = x_ref[:, pl.ds(at, 256)].T
        return carry

    lax.fori_loop(0, WIDTH // 256, one, 0)
    core = core_ref[0]

    def give(b, carry):
        for ref, k in ((own_ref, core), (other_ref, 1 - core)):
            start = pl.multiple_of((b * CORES + k) * ROWS, ROWS)
            ref[b] = turned[pl.ds(start, ROWS), :]
        return carry

    lax.fori_loop(0, Z_HI * Y, give, 0)


def turn(core, x, step, after):
    shape = jax.ShapeDtypeStruct((Z_HI * Y, ROWS, TOK), jnp.bfloat16)
    return pl.pallas_call(
        turn_kernel,
        grid_spec=pltpu.PrefetchScalarGridSpec(
            num_scalar_prefetch=1,
            grid=(1,),
            in_specs=[pl.BlockSpec((None, None, TOK, WIDTH), lambda i, s: (step, 0, 0, 0))]
            + [pl.BlockSpec(memory_space=pl.ANY)] * len(after),
            out_specs=[pl.BlockSpec((Z_HI * Y, ROWS, TOK), lambda i, s: (0, 0, 0))] * 2,
            scratch_shapes=[pltpu.VMEM((WIDTH, TOK), jnp.bfloat16)],
        ),
        out_shape=[shape, shape],
        compiler_params=PARAMS,
        cost_estimate=SMALL,
    )(core, x, *after)


def products_kernel(adds, layout, terms, tiles, blocks_ref, *refs):
    units = len(adds)
    own, other = refs[:units], refs[units : 2 * units]
    at = 2 * units + 2 * tiles
    y_own, y_other = refs[2 * units : at - tiles], refs[at - tiles : at]
    given = [refs[at + t * tiles : at + (t + 1) * tiles] for t in range(terms)]
    outs = refs[len(refs) - len(layout) :]
    x = jnp.concatenate(
        [jnp.concatenate([a[0], b[0]], axis=1) for a, b in zip(own, other)], axis=0
    )
    total = jnp.concatenate(
        [
            jnp.dot(
                x,
                jnp.concatenate([a[...], b[...]], axis=0),
                preferred_element_type=jnp.float32,
            )
            for a, b in zip(y_own, y_other)
        ],
        axis=1,
    )
    parts = []
    for u, per_unit in enumerate(adds):
        part = total[u * ROWS : (u + 1) * ROWS]
        for term, plane in per_unit:
            more = jnp.concatenate([r[plane] for r in given[term]], axis=1)
            part = part + more.astype(jnp.float32)
        parts.append(part)
    for out, planes in zip(outs, layout):
        for p, u in enumerate(planes):
            out[p] = parts[u].astype(out.dtype)


def products(pair, step, chunk, blocks, adds, terms, layout, dtypes, after=()):
    x_own, x_other, y_own, y_other = pair
    column, width = chunk
    units = len(adds)
    x_specs = [
        pl.BlockSpec((1, ROWS, TOK), lambda j, s, u=u: (s[u], 0, 0)) for u in range(units)
    ]
    tiles = width // TILE
    y_specs = [
        pl.BlockSpec((None, None, TOK, TILE), lambda j, s, t=t: (step, 0, 0, column // TILE + t))
        for t in range(tiles)
    ]

    t_specs = [
        pl.BlockSpec((t.shape[0], ROWS, TILE), lambda j, s, k=first // TILE + k: (0, 0, k))
        for t, first in terms
        for k in range(tiles)
    ]
    outs = [(len(planes), ROWS, width) for planes in layout]
    return pl.pallas_call(
        partial(products_kernel, adds, layout, len(terms), tiles),
        grid_spec=pltpu.PrefetchScalarGridSpec(
            num_scalar_prefetch=1,
            grid=(1,),
            in_specs=x_specs * 2
            + y_specs * 2
            + t_specs
            + [pl.BlockSpec(memory_space=pl.ANY)] * len(after),
            out_specs=[pl.BlockSpec(o, lambda j, s: (0, 0, 0)) for o in outs],
        ),
        out_shape=[jax.ShapeDtypeStruct(o, d) for o, d in zip(outs, dtypes)],
        compiler_params=PARAMS,
        cost_estimate=SMALL,
    )(blocks, *([x_own] * units), *([x_other] * units), *([y_own] * tiles), *([y_other] * tiles), *(t for t, _ in terms for _ in range(tiles)), *after)


def strips(work):
    def one(i, carry):
        work(pl.ds(pl.multiple_of(i * STRIP, STRIP), STRIP))
        return carry

    lax.fori_loop(0, ROWS // STRIP, one, 0)


def by_columns(kernel, ins, outs, width, after=(), into=None):
    def spec(array, column, plane=0):
        lead = (None,) * (len(array.shape) - 2)
        return pl.BlockSpec(
            (*lead, ROWS, TILE), lambda j: (*(plane for _ in lead), 0, column // TILE + j)
        )

    shapes = [jax.ShapeDtypeStruct((ROWS, columns), dtype) for columns, _, dtype in outs]
    unread = list(after)
    aliases = {}
    if into is not None:
        aliases = {len(ins) + len(unread): len(outs) - 1}
        unread.append(into)

    def body(*refs):
        used = refs[: len(ins)] + refs[len(ins) + len(unread) :]
        strips(partial(kernel, *used))

    return pl.pallas_call(
        body,
        grid=(width // TILE,),
        in_specs=[spec(*i) for i in ins] + [pl.BlockSpec(memory_space=pl.ANY)] * len(unread),
        out_specs=[spec(shape, o[1]) for shape, o in zip(shapes, outs)],
        out_shape=shapes,
        input_output_aliases=aliases,
        compiler_params=PARAMS,
        cost_estimate=SMALL,
    )(*(i[0] for i in ins), *unread)


def adam(params, first, second, gradient):
    first = BETA_ONE * first + (1.0 - BETA_ONE) * gradient
    second = BETA_TWO * second + (1.0 - BETA_TWO) * gradient * gradient
    updated = params - LEARN_RATE * (first / (jnp.sqrt(second) + EPSILON) + WEIGHT_DECAY * params)
    return first, second, updated.astype(jnp.bfloat16)


def average(own, partner):
    return ((own.astype(jnp.float32) + partner.astype(jnp.float32)) * 0.5).astype(jnp.bfloat16)


def gradient_of(terms, at):
    total = terms[0][at].astype(jnp.float32)
    for term in terms[1:]:
        total = total + term[at].astype(jnp.float32)
    return total


def first_kernel(w, m, v, *rest):
    *terms, new_m, new_v, new_u, at = rest
    f32 = jnp.float32
    new_m[at], new_v[at], new_u[at] = adam(
        w[at].astype(f32), m[at].astype(f32), v[at].astype(f32), gradient_of(terms, at)
    )


def second_kernel(own, partner, m, v, *rest):
    *terms, new_u, new_m, at = rest
    w = average(own[at], partner[at]).astype(jnp.float32)
    new_m[at], _, new_u[at] = adam(w, m[at], v[at], gradient_of(terms, at))


def give_kernel(own, up, down, out, at):
    out[at] = gradient_of((own, up, down), at).astype(out.dtype)


def average_kernel(own, partner, out, at):
    out[at] = average(own[at], partner[at])


def per_device(x, y, weight, first, second, step_index):
    levels = [(step_index[0] + s) % LEVELS for s in range(2)]
    index = lax.axis_index("fsdp")
    core, at_y, at_z = index % CORES, (index // CORES) % Y, index // (Y * CORES)
    bf16, f32 = jnp.bfloat16, jnp.float32

    def chosen(*pairs):
        rows = [((at_z + dz) % Z_HI) * Y + (at_y + dy) % Y for dy, dz in pairs]
        return jnp.stack(rows).astype(jnp.int32)

    core = core.astype(jnp.int32)[None]
    y_other = core_swap(y)
    last = []
    pairs = []
    for s in range(2):
        x_own, x_give = turn(core, x, s, tuple(last))
        last[:] = [x_own]
        pairs.append((x_own, core_swap(x_give), y, y_other))

    def go(step, chunk, blocks, adds, terms, layout, after=()):
        outs = products(
            pairs[step],
            step,
            chunk,
            chosen(*blocks),
            adds,
            terms,
            layout,
            (bf16,) * len(layout),
            (*last, *after),
        )
        last[:] = [outs[0]]
        return outs

    def far(step, chunk):
        up, down = go(step, chunk, ((2, 0), (2, 1)), ((), ()), (), ((0,), (1,)))
        return y_move(up, 1), y_move(down, -1)

    def near(step, chunk, arrived, after=()):
        up, down, mine, other = go(
            step,
            chunk,
            ((1, 0), (1, 1), (-1, 0), (-1, 1), (0, 0), (0, 1)),
            (((0, 0),), (), (), ((1, 0),), (), ()),
            [(t, chunk[0]) for t in arrived],
            ((0, 1), (2, 3), (4,), (5,)),
            after,
        )
        return y_move(up, 1), y_move(down, -1), mine, other

    def follow(kernel, ins, outs, width, into=None):
        results = by_columns(kernel, ins, outs, width, tuple(last), into)
        last[:] = [results[0]]
        return results

    def across(chunk, sums):
        up, down, mine, other = sums
        (give,) = follow(
            give_kernel,
            [(other, 0), (up, 0, 1), (down, 0, 1)],
            [(chunk[1], 0, bf16)],
            chunk[1],
        )
        return [(mine, 0), (up, 0), (down, 0), (z_swap(give), 0)]

    def first_step(chunk, terms):
        column, width = chunk
        m, v, u = follow(
            first_kernel,
            [(weight, column), (first, column), (second, column)] + terms,
            [(width, 0, f32), (width, 0, f32), (width, 0, bf16)],
            width,
        )
        partner = group_move(levels[0], u)
        last[:] = [partner]
        return u, partner, m, v

    def second_step(chunk, state, terms, moments):
        column, width = chunk
        u, moments = follow(
            second_kernel,
            [(t, 0) for t in state] + terms,
            [(width, 0, bf16), (WIDTH, column, f32)],
            width,
            moments,
        )
        partner = group_move(levels[1], u)
        last[:] = [partner]
        return (u, partner), moments

    def finish(chunk, both, weights):
        column, width = chunk
        (weights,) = follow(
            average_kernel, [(t, 0) for t in both], [(WIDTH, column, bf16)], width, weights
        )
        return weights

    a, b = CHUNKS
    far_ab = far(0, (0, WIDTH))
    near_a = near(0, a, far_ab)
    far_cd = far(1, (0, WIDTH))
    terms_a = across(a, near_a)
    near_b = near(0, b, far_ab)
    near_c = near(1, a, far_cd)
    state_a = first_step(a, terms_a)
    terms_b = across(b, near_b)
    near_d = near(1, b, far_cd)
    terms_c = across(a, near_c)
    state_b = first_step(b, terms_b)
    terms_d = across(b, near_d)
    both_c, moments = second_step(a, state_a, terms_c, None)
    weights = finish(a, both_c, None)
    both_d, moments = second_step(b, state_b, terms_d, moments)
    weights = finish(b, both_d, weights)
    return weights[None], moments[None]


def solution(mesh):
    in_specs = (
        P(None, "group", "fsdp", None),
        P(None, "group", "fsdp", None),
        P("group", "fsdp", None),
        P("group", "fsdp", None),
        P("group", "fsdp", None),
        P(),
    )
    out_specs = (P("group", "fsdp", None), P("group", "fsdp", None))
    return jax.shard_map(
        per_device, mesh=mesh, in_specs=in_specs, out_specs=out_specs, check_vma=False
    )
```

```python
from functools import partial

import jax
import jax.numpy as jnp
from jax import lax
from jax.experimental import pallas as pl
from jax.experimental.pallas import tpu as pltpu
from jax.sharding import PartitionSpec as P

LEARN_RATE = 0.05
WEIGHT_DECAY = 0.1
BETA_ONE = 0.9
BETA_TWO = 0.95
EPSILON = 1e-08

Z_HI, Y, CORES = 2, 4, 2
N_FSDP = Z_HI * Y * CORES
N_GROUP = 16
LEVELS = N_GROUP.bit_length() - 1
ROWS = 160
TOK = 384
WIDTH = 2560
CHUNKS = ((0, 1280), (1280, 1280))
TILE = 1280
STRIP = 16
SMALL = pl.CostEstimate(flops=1024, bytes_accessed=1024, transcendentals=0)
PARAMS = pltpu.CompilerParams(vmem_limit_bytes=32 * 1024 * 1024)


def held(array):
    return pltpu.with_memory_space_constraint(array, pltpu.HBM)


def fsdp_move(block, move):
    def target(i):
        z, y, c = i // (Y * CORES), (i // CORES) % Y, i % CORES
        z, y, c = move(z, y, c)
        return ((z % Z_HI) * Y + y % Y) * CORES + c % CORES

    return lax.ppermute(block, "fsdp", [(i, target(i)) for i in range(N_FSDP)])


def y_move(block, shift):
    return fsdp_move(block, lambda z, y, c: (z, y + shift, c))


def z_swap(block):
    return fsdp_move(block, lambda z, y, c: (z + 1, y, c))


def core_swap(block):
    return fsdp_move(block, lambda z, y, c: (z, y, c + 1))


def group_move(level, block):
    def moved(distance, block):
        return lax.ppermute(
            block, "group", [((i - distance) % N_GROUP, i) for i in range(N_GROUP)]
        )

    return lax.switch(level, [partial(moved, 1 << k) for k in range(LEVELS)], block)


def turn_kernel(core_ref, x_ref, *refs):
    own_ref, other_ref, turned = refs[-3:]

    def one(j, carry):
        at = pl.multiple_of(j * 256, 256)
        turned[pl.ds(at, 256), :] = x_ref[:, pl.ds(at, 256)].T
        return carry

    lax.fori_loop(0, WIDTH // 256, one, 0)
    core = core_ref[0]

    def give(b, carry):
        for ref, k in ((own_ref, core), (other_ref, 1 - core)):
            start = pl.multiple_of((b * CORES + k) * ROWS, ROWS)
            ref[b] = turned[pl.ds(start, ROWS), :]
        return carry

    lax.fori_loop(0, Z_HI * Y, give, 0)


def turn(core, x, step, after):
    shape = (Z_HI * Y, ROWS, TOK)
    return pl.pallas_call(
        turn_kernel,
        grid_spec=pltpu.PrefetchScalarGridSpec(
            num_scalar_prefetch=1,
            grid=(1,),
            in_specs=[pl.BlockSpec((None, None, TOK, WIDTH), lambda i, s: (step, 0, 0, 0))]
            + [pl.BlockSpec(memory_space=pl.ANY)] * len(after),
            out_specs=[pl.BlockSpec((Z_HI * Y, ROWS, TOK), lambda i, s: (0, 0, 0))] * 2,
            scratch_shapes=[pltpu.VMEM((WIDTH, TOK), jnp.bfloat16)],
        ),
        out_shape=[
            pltpu.HBM(shape, jnp.bfloat16),
            jax.ShapeDtypeStruct(shape, jnp.bfloat16),
        ],
        compiler_params=PARAMS,
        cost_estimate=SMALL,
    )(core, held(x), *after)


def products_kernel(adds, layout, terms, tiles, blocks_ref, *refs):
    units = len(adds)
    own, other = refs[:units], refs[units : 2 * units]
    at = 2 * units + 2 * tiles
    y_own, y_other = refs[2 * units : at - tiles], refs[at - tiles : at]
    given = [refs[at + t * tiles : at + (t + 1) * tiles] for t in range(terms)]
    outs = refs[len(refs) - len(layout) :]
    x = jnp.concatenate(
        [jnp.concatenate([a[0], b[0]], axis=1) for a, b in zip(own, other)], axis=0
    )
    total = jnp.concatenate(
        [
            jnp.dot(
                x,
                jnp.concatenate([a[...], b[...]], axis=0),
                preferred_element_type=jnp.float32,
            )
            for a, b in zip(y_own, y_other)
        ],
        axis=1,
    )
    parts = []
    for u, per_unit in enumerate(adds):
        part = total[u * ROWS : (u + 1) * ROWS]
        for term, plane in per_unit:
            more = jnp.concatenate([r[plane] for r in given[term]], axis=1)
            part = part + more.astype(jnp.float32)
        parts.append(part)
    for out, planes in zip(outs, layout):
        for p, u in enumerate(planes):
            out[p] = parts[u].astype(out.dtype)


def products(pair, step, chunk, blocks, adds, terms, layout, dtypes, after=()):
    x_own, x_other, y_own, y_other = pair
    column, width = chunk
    units = len(adds)
    x_specs = [
        pl.BlockSpec((1, ROWS, TOK), lambda j, s, u=u: (s[u], 0, 0)) for u in range(units)
    ]
    tiles = width // TILE
    y_specs = [
        pl.BlockSpec((None, None, TOK, TILE), lambda j, s, t=t: (step, 0, 0, column // TILE + t))
        for t in range(tiles)
    ]

    t_specs = [
        pl.BlockSpec((t.shape[0], ROWS, TILE), lambda j, s, k=first // TILE + k: (0, 0, k))
        for t, first in terms
        for k in range(tiles)
    ]
    outs = [(len(planes), ROWS, width) for planes in layout]
    return pl.pallas_call(
        partial(products_kernel, adds, layout, len(terms), tiles),
        grid_spec=pltpu.PrefetchScalarGridSpec(
            num_scalar_prefetch=1,
            grid=(1,),
            in_specs=x_specs * 2
            + y_specs * 2
            + t_specs
            + [pl.BlockSpec(memory_space=pl.ANY)] * len(after),
            out_specs=[pl.BlockSpec(o, lambda j, s: (0, 0, 0)) for o in outs],
        ),
        out_shape=[
            jax.ShapeDtypeStruct(o, d) if i < 2 else pltpu.HBM(o, d)
            for i, (o, d) in enumerate(zip(outs, dtypes))
        ],
        compiler_params=PARAMS,
        cost_estimate=SMALL,
    )(
        blocks,
        *([held(x_own)] * units),
        *([x_other] * units),
        *([held(y_own)] * tiles),
        *([held(y_other)] * tiles),
        *(t for t, _ in terms for _ in range(tiles)),
        *after,
    )


def strips(work):
    def one(i, carry):
        work(pl.ds(pl.multiple_of(i * STRIP, STRIP), STRIP))
        return carry

    lax.fori_loop(0, ROWS // STRIP, one, 0)


def by_columns(kernel, ins, outs, width, after=(), into=None):
    def spec(array, column, plane=0):
        lead = (None,) * (len(array.shape) - 2)
        return pl.BlockSpec(
            (*lead, ROWS, TILE), lambda j: (*(plane for _ in lead), 0, column // TILE + j)
        )

    shapes = [
        (pltpu.HBM if dtype == jnp.float32 or columns == WIDTH else jax.ShapeDtypeStruct)(
            (ROWS, columns), dtype
        )
        for columns, _, dtype in outs
    ]
    unread = list(after)
    aliases = {}
    if into is not None:
        aliases = {len(ins) + len(unread): len(outs) - 1}
        unread.append(held(into))

    def body(*refs):
        used = refs[: len(ins)] + refs[len(ins) + len(unread) :]
        strips(partial(kernel, *used))

    return pl.pallas_call(
        body,
        grid=(width // TILE,),
        in_specs=[spec(*i) for i in ins] + [pl.BlockSpec(memory_space=pl.ANY)] * len(unread),
        out_specs=[spec(shape, o[1]) for shape, o in zip(shapes, outs)],
        out_shape=shapes,
        input_output_aliases=aliases,
        compiler_params=PARAMS,
        cost_estimate=SMALL,
    )(*(i[0] for i in ins), *unread)


def adam(params, first, second, gradient):
    first = BETA_ONE * first + (1.0 - BETA_ONE) * gradient
    second = BETA_TWO * second + (1.0 - BETA_TWO) * gradient * gradient
    updated = params - LEARN_RATE * (first / (jnp.sqrt(second) + EPSILON) + WEIGHT_DECAY * params)
    return first, second, updated.astype(jnp.bfloat16)


def average(own, partner):
    return ((own.astype(jnp.float32) + partner.astype(jnp.float32)) * 0.5).astype(jnp.bfloat16)


def gradient_of(terms, at):
    total = terms[0][at].astype(jnp.float32)
    for term in terms[1:]:
        total = total + term[at].astype(jnp.float32)
    return total


def first_kernel(w, m, v, *rest):
    *terms, new_m, new_v, new_u, at = rest
    f32 = jnp.float32
    new_m[at], new_v[at], new_u[at] = adam(
        w[at].astype(f32), m[at].astype(f32), v[at].astype(f32), gradient_of(terms, at)
    )


def second_kernel(own, partner, m, v, *rest):
    *terms, new_u, new_m, at = rest
    w = average(own[at], partner[at]).astype(jnp.float32)
    new_m[at], _, new_u[at] = adam(w, m[at], v[at], gradient_of(terms, at))


def give_kernel(mine, mine_up, mine_down, other, up, down, total, give, at):
    total[at] = gradient_of((mine, mine_up, mine_down), at)
    give[at] = gradient_of((other, up, down), at).astype(give.dtype)


def average_kernel(own, partner, out, at):
    out[at] = average(own[at], partner[at])


def per_device(x, y, weight, first, second, step_index):
    levels = [(step_index[0] + s) % LEVELS for s in range(2)]
    index = lax.axis_index("fsdp")
    core, at_y, at_z = index % CORES, (index // CORES) % Y, index // (Y * CORES)
    bf16, f32 = jnp.bfloat16, jnp.float32

    def chosen(*pairs):
        rows = [((at_z + dz) % Z_HI) * Y + (at_y + dy) % Y for dy, dz in pairs]
        return jnp.stack(rows).astype(jnp.int32)

    core = core.astype(jnp.int32)[None]
    y_other = core_swap(y)
    last = []
    pairs = []
    for s in range(2):
        x_own, x_give = turn(core, x, s, tuple(last))
        last[:] = [held(x_own)]
        pairs.append((x_own, core_swap(x_give), y, y_other))

    def go(step, chunk, blocks, adds, terms, layout, after=()):
        outs = products(
            pairs[step],
            step,
            chunk,
            chosen(*blocks),
            adds,
            terms,
            layout,
            (bf16,) * len(layout),
            (*last, *after),
        )
        last[:] = [outs[0]]
        return outs

    def far(step, chunk):
        up, down = go(step, chunk, ((2, 0), (2, 1)), ((), ()), (), ((0,), (1,)))
        return y_move(up, 1), y_move(down, -1)

    def near(step, chunk, arrived, after=()):
        up, down, mine, other = go(
            step,
            chunk,
            ((1, 0), (1, 1), (-1, 0), (-1, 1), (0, 0), (0, 1)),
            (((0, 0),), (), (), ((1, 0),), (), ()),
            [(t, chunk[0]) for t in arrived],
            ((0, 1), (2, 3), (4,), (5,)),
            after,
        )
        return y_move(up, 1), y_move(down, -1), mine, other

    def follow(kernel, ins, outs, width, into=None):
        results = by_columns(kernel, ins, outs, width, tuple(last), into)
        last[:] = [held(results[0]) if outs[0][2] == f32 or outs[0][0] == WIDTH else results[0]]
        return results

    def across(chunk, sums):
        up, down, mine, other = sums
        total, give = follow(
            give_kernel,
            [(held(mine), 0), (up, 0), (down, 0), (held(other), 0), (up, 0, 1), (down, 0, 1)],
            [(chunk[1], 0, f32), (chunk[1], 0, bf16)],
            chunk[1],
        )
        return [(held(total), 0), (z_swap(give), 0)]

    def first_step(chunk, terms, u):
        column, width = chunk
        m, v, u = follow(
            first_kernel,
            [(held(t), column) for t in (weight, first, second)] + terms,
            [(width, 0, f32), (width, 0, f32), (WIDTH, column, bf16)],
            width,
            u,
        )
        return m, v, u

    def second_step(chunk, state, terms, moments):
        column, width = chunk
        m, v = state
        u, moments = follow(
            second_kernel,
            [(held(updated), column), (partner, column), (held(m), 0), (held(v), 0)] + terms,
            [(width, 0, bf16), (WIDTH, column, f32)],
            width,
            moments,
        )
        partner_u = group_move(levels[1], u)
        last[:] = [partner_u]
        return (u, partner_u), moments

    def finish(chunk, both, weights):
        column, width = chunk
        (weights,) = follow(
            average_kernel, [(t, 0) for t in both], [(WIDTH, column, bf16)], width, weights
        )
        return weights

    a, b = CHUNKS
    far_ab = far(0, (0, WIDTH))
    near_a = near(0, a, far_ab)
    far_cd = far(1, (0, WIDTH))
    terms_a = across(a, near_a)
    near_b = near(0, b, far_ab)
    near_c = near(1, a, far_cd)
    terms_b = across(b, near_b)
    *state_a, updated = first_step(a, terms_a, None)
    near_d = near(1, b, far_cd)
    terms_c = across(a, near_c)
    *state_b, updated = first_step(b, terms_b, updated)
    partner = group_move(levels[0], updated)
    last[:] = [partner]
    terms_d = across(b, near_d)
    both_c, moments = second_step(a, state_a, terms_c, None)
    weights = finish(a, both_c, None)
    both_d, moments = second_step(b, state_b, terms_d, moments)
    weights = finish(b, both_d, weights)
    return weights[None], moments[None]


def solution(mesh):
    in_specs = (
        P(None, "group", "fsdp", None),
        P(None, "group", "fsdp", None),
        P("group", "fsdp", None),
        P("group", "fsdp", None),
        P("group", "fsdp", None),
        P(),
    )
    out_specs = (P("group", "fsdp", None), P("group", "fsdp", None))
    return jax.shard_map(
        per_device, mesh=mesh, in_specs=in_specs, out_specs=out_specs, check_vma=False
    )
```

```python
from functools import partial

import jax
import jax.numpy as jnp
from jax import lax
from jax.experimental import pallas as pl
from jax.experimental.pallas import tpu as pltpu
from jax.sharding import PartitionSpec as P

LEARN_RATE = 0.05
WEIGHT_DECAY = 0.1
BETA_ONE = 0.9
BETA_TWO = 0.95
EPSILON = 1e-08

Z_HI, Y, CORES = 2, 4, 2
N_FSDP = Z_HI * Y * CORES
N_GROUP = 16
LEVELS = N_GROUP.bit_length() - 1
ROWS = 160
TOK = 384
WIDTH = 2560
CHUNKS = ((0, 1280), (1280, 1280))
TILE = 1280
STRIP = 16
SMALL = pl.CostEstimate(flops=1024, bytes_accessed=1024, transcendentals=0)
PARAMS = pltpu.CompilerParams(vmem_limit_bytes=32 * 1024 * 1024)


def held(array):
    return pltpu.with_memory_space_constraint(array, pltpu.HBM)


def fsdp_move(block, move):
    def target(i):
        z, y, c = i // (Y * CORES), (i // CORES) % Y, i % CORES
        z, y, c = move(z, y, c)
        return ((z % Z_HI) * Y + y % Y) * CORES + c % CORES

    return lax.ppermute(block, "fsdp", [(i, target(i)) for i in range(N_FSDP)])


def y_move(block, shift):
    return fsdp_move(block, lambda z, y, c: (z, y + shift, c))


def z_swap(block):
    return fsdp_move(block, lambda z, y, c: (z + 1, y, c))


def core_swap(block):
    return fsdp_move(block, lambda z, y, c: (z, y, c + 1))


def group_move(block, distance):
    return lax.ppermute(
        block, "group", [((i - distance) % N_GROUP, i) for i in range(N_GROUP)]
    )


def turn_kernel(core_ref, x_ref, *refs):
    own_ref, other_ref, turned = refs[-3:]

    def one(j, carry):
        at = pl.multiple_of(j * 256, 256)
        turned[pl.ds(at, 256), :] = x_ref[:, pl.ds(at, 256)].T
        return carry

    lax.fori_loop(0, WIDTH // 256, one, 0)
    core = core_ref[0]

    def give(b, carry):
        for ref, k in ((own_ref, core), (other_ref, 1 - core)):
            start = pl.multiple_of((b * CORES + k) * ROWS, ROWS)
            ref[b] = turned[pl.ds(start, ROWS), :]
        return carry

    lax.fori_loop(0, Z_HI * Y, give, 0)


def turn(core, x, step, after):
    shape = jax.ShapeDtypeStruct((Z_HI * Y, ROWS, TOK), jnp.bfloat16)
    return pl.pallas_call(
        turn_kernel,
        grid_spec=pltpu.PrefetchScalarGridSpec(
            num_scalar_prefetch=1,
            grid=(1,),
            in_specs=[pl.BlockSpec((None, None, TOK, WIDTH), lambda i, s: (step, 0, 0, 0))]
            + [pl.BlockSpec(memory_space=pl.ANY)] * len(after),
            out_specs=[pl.BlockSpec((Z_HI * Y, ROWS, TOK), lambda i, s: (0, 0, 0))] * 2,
            scratch_shapes=[pltpu.VMEM((WIDTH, TOK), jnp.bfloat16)],
        ),
        out_shape=[shape, shape],
        compiler_params=PARAMS,
        cost_estimate=SMALL,
    )(core, held(x), *after)


def products_kernel(adds, layout, terms, tiles, blocks_ref, *refs):
    units = len(adds)
    own, other = refs[:units], refs[units : 2 * units]
    at = 2 * units + 2 * tiles
    y_own, y_other = refs[2 * units : at - tiles], refs[at - tiles : at]
    given = [refs[at + t * tiles : at + (t + 1) * tiles] for t in range(terms)]
    outs = refs[len(refs) - len(layout) :]
    x = jnp.concatenate(
        [jnp.concatenate([a[0], b[0]], axis=1) for a, b in zip(own, other)], axis=0
    )
    total = jnp.concatenate(
        [
            jnp.dot(
                x,
                jnp.concatenate([a[...], b[...]], axis=0),
                preferred_element_type=jnp.float32,
            )
            for a, b in zip(y_own, y_other)
        ],
        axis=1,
    )
    parts = []
    for u, per_unit in enumerate(adds):
        part = total[u * ROWS : (u + 1) * ROWS]
        for term, plane in per_unit:
            more = jnp.concatenate([r[plane] for r in given[term]], axis=1)
            part = part + more.astype(jnp.float32)
        parts.append(part)
    for out, planes in zip(outs, layout):
        for p, u in enumerate(planes):
            out[p] = parts[u].astype(out.dtype)


def products(pair, step, chunk, blocks, adds, terms, layout, dtypes, after=(), hold=False):
    x_own, x_other, y_own, y_other = pair
    if hold:
        y_own, y_other = held(y_own), held(y_other)
    column, width = chunk
    units = len(adds)
    x_specs = [
        pl.BlockSpec((1, ROWS, TOK), lambda j, s, u=u: (s[u], 0, 0)) for u in range(units)
    ]
    tiles = width // TILE
    y_specs = [
        pl.BlockSpec((None, None, TOK, TILE), lambda j, s, t=t: (step, 0, 0, column // TILE + t))
        for t in range(tiles)
    ]

    t_specs = [
        pl.BlockSpec((t.shape[0], ROWS, TILE), lambda j, s, k=first // TILE + k: (0, 0, k))
        for t, first in terms
        for k in range(tiles)
    ]
    outs = [(len(planes), ROWS, width) for planes in layout]
    return pl.pallas_call(
        partial(products_kernel, adds, layout, len(terms), tiles),
        grid_spec=pltpu.PrefetchScalarGridSpec(
            num_scalar_prefetch=1,
            grid=(1,),
            in_specs=x_specs * 2
            + y_specs * 2
            + t_specs
            + [pl.BlockSpec(memory_space=pl.ANY)] * len(after),
            out_specs=[pl.BlockSpec(o, lambda j, s: (0, 0, 0)) for o in outs],
        ),
        out_shape=[jax.ShapeDtypeStruct(o, d) for o, d in zip(outs, dtypes)],
        compiler_params=PARAMS,
        cost_estimate=SMALL,
    )(
        blocks,
        *([x_own] * units),
        *([x_other] * units),
        *([y_own] * tiles),
        *([y_other] * tiles),
        *(t for t, _ in terms for _ in range(tiles)),
        *after,
    )


def strips(work):
    def one(i, carry):
        work(pl.ds(pl.multiple_of(i * STRIP, STRIP), STRIP))
        return carry

    lax.fori_loop(0, ROWS // STRIP, one, 0)


def by_columns(kernel, ins, outs, width, after=(), into=None):
    def spec(array, column, plane=0):
        lead = (None,) * (len(array.shape) - 2)
        return pl.BlockSpec(
            (*lead, ROWS, TILE), lambda j: (*(plane for _ in lead), 0, column // TILE + j)
        )

    shapes = [jax.ShapeDtypeStruct((ROWS, columns), dtype) for columns, _, dtype in outs]
    unread = list(after)
    aliases = {}
    if into is not None:
        aliases = {len(ins) + len(unread): len(outs) - 1}
        unread.append(into)

    def body(*refs):
        used = refs[: len(ins)] + refs[len(ins) + len(unread) :]
        strips(partial(kernel, *used))

    return pl.pallas_call(
        body,
        grid=(width // TILE,),
        in_specs=[spec(*i) for i in ins] + [pl.BlockSpec(memory_space=pl.ANY)] * len(unread),
        out_specs=[spec(shape, o[1]) for shape, o in zip(shapes, outs)],
        out_shape=shapes,
        input_output_aliases=aliases,
        compiler_params=PARAMS,
        cost_estimate=SMALL,
    )(*(i[0] for i in ins), *unread)


def adam(params, first, second, gradient):
    first = BETA_ONE * first + (1.0 - BETA_ONE) * gradient
    second = BETA_TWO * second + (1.0 - BETA_TWO) * gradient * gradient
    updated = params - LEARN_RATE * (first / (jnp.sqrt(second) + EPSILON) + WEIGHT_DECAY * params)
    return first, second, updated.astype(jnp.bfloat16)


def average(own, partner):
    return ((own.astype(jnp.float32) + partner.astype(jnp.float32)) * 0.5).astype(jnp.bfloat16)


def gradient_of(terms, at):
    total = terms[0][at].astype(jnp.float32)
    for term in terms[1:]:
        total = total + term[at].astype(jnp.float32)
    return total


def first_kernel(w, m, v, *rest):
    *terms, new_m, new_v, new_u, at = rest
    f32 = jnp.float32
    new_m[at], new_v[at], new_u[at] = adam(
        w[at].astype(f32), m[at].astype(f32), v[at].astype(f32), gradient_of(terms, at)
    )


def second_kernel(own, partner, m, v, *rest):
    *terms, new_u, new_m, at = rest
    w = average(own[at], partner[at]).astype(jnp.float32)
    new_m[at], _, new_u[at] = adam(w, m[at], v[at], gradient_of(terms, at))


def give_kernel(mine, mine_up, mine_down, other, up, down, total, give, at):
    total[at] = gradient_of((mine, mine_up, mine_down), at)
    give[at] = gradient_of((other, up, down), at).astype(give.dtype)


def average_kernel(own, partner, out, at):
    out[at] = average(own[at], partner[at])


def per_device(x, y, weight, first, second, step_index):
    index = lax.axis_index("fsdp")
    core, at_y, at_z = index % CORES, (index // CORES) % Y, index // (Y * CORES)
    bf16, f32 = jnp.bfloat16, jnp.float32

    def chosen(*pairs):
        rows = [((at_z + dz) % Z_HI) * Y + (at_y + dy) % Y for dy, dz in pairs]
        return jnp.stack(rows).astype(jnp.int32)

    core = core.astype(jnp.int32)[None]
    y_other = core_swap(y)
    last = []
    pairs = []
    for s in range(2):
        x_own, x_give = turn(core, x, s, tuple(last))
        last[:] = [x_own]
        pairs.append((x_own, core_swap(x_give), y, y_other))

    def go(step, chunk, blocks, adds, terms, layout, hold=False):
        outs = products(
            pairs[step],
            step,
            chunk,
            chosen(*blocks),
            adds,
            terms,
            layout,
            (bf16,) * len(layout),
            tuple(last),
            hold,
        )
        last[:] = [outs[0]]
        return outs

    def far(step, chunk):
        up, down = go(step, chunk, ((2, 0), (2, 1)), ((), ()), (), ((0,), (1,)), step == 0)
        return y_move(up, 1), y_move(down, -1)

    def near(step, chunk, arrived):
        up, down, mine, other = go(
            step,
            chunk,
            ((1, 0), (1, 1), (-1, 0), (-1, 1), (0, 0), (0, 1)),
            (((0, 0),), (), (), ((1, 0),), (), ()),
            [(t, chunk[0]) for t in arrived],
            ((0, 1), (2, 3), (4,), (5,)),
        )
        return y_move(up, 1), y_move(down, -1), mine, other

    def follow(kernel, ins, outs, width, into=None):
        results = by_columns(kernel, ins, outs, width, tuple(last), into)
        last[:] = [results[0]]
        return results

    def across(chunk, sums):
        up, down, mine, other = sums
        return follow(
            give_kernel,
            [(mine, 0), (up, 0), (down, 0), (other, 0), (up, 0, 1), (down, 0, 1)],
            [(chunk[1], 0, f32), (chunk[1], 0, bf16)],
            chunk[1],
        )

    def first_step(chunk, total, give):
        column, width = chunk
        return follow(
            first_kernel,
            [(t, column) for t in (weight, first, second)] + [(total, 0), (z_swap(give), 0)],
            [(width, 0, f32), (width, 0, f32), (width, 0, bf16)],
            width,
        )

    a, b = CHUNKS
    far_ab = far(0, (0, WIDTH))
    near_a = near(0, a, far_ab)
    far_cd = far(1, (0, WIDTH))
    sums_a = across(a, near_a)
    near_b = near(0, b, far_ab)
    near_c = near(1, a, far_cd)
    sums_b = across(b, near_b)
    state_a = first_step(a, *sums_a)
    near_d = near(1, b, far_cd)
    total_c, give_c = across(a, near_c)
    state_b = first_step(b, *sums_b)
    total_d, give_d = across(b, near_d)
    return lax.switch(
        step_index[0] % LEVELS,
        [partial(ending, level) for level in range(LEVELS)],
        state_a,
        state_b,
        total_c,
        total_d,
        z_swap(give_c),
        give_d,
    )


def ending(level, state_a, state_b, total_c, total_d, got_c, give_d):
    distances = 1 << level, 1 << ((level + 1) % LEVELS)
    bf16, f32 = jnp.bfloat16, jnp.float32
    partners = [group_move(state[2], distances[0]) for state in (state_a, state_b)]
    gots = got_c, z_swap(give_d)
    moments, after, boths = None, (), []
    for chunk, state, partner, total, got in zip(
        CHUNKS, (state_a, state_b), partners, (total_c, total_d), gots
    ):
        column, width = chunk
        m, v, u = state
        u, moments = by_columns(
            second_kernel,
            [(t, 0) for t in (u, partner, m, v, total, got)],
            [(width, 0, bf16), (WIDTH, column, f32)],
            width,
            after,
            moments,
        )
        after = (u,)
        boths.append((u, group_move(u, distances[1])))
    weights = None
    for (column, width), both in zip(CHUNKS, boths):
        (weights,) = by_columns(
            average_kernel, [(t, 0) for t in both], [(WIDTH, column, bf16)], width, after, weights
        )
        after = ()
    return weights[None], moments[None]


def solution(mesh):
    in_specs = (
        P(None, "group", "fsdp", None),
        P(None, "group", "fsdp", None),
        P("group", "fsdp", None),
        P("group", "fsdp", None),
        P("group", "fsdp", None),
        P(),
    )
    out_specs = (P("group", "fsdp", None), P("group", "fsdp", None))
    return jax.shard_map(
        per_device, mesh=mesh, in_specs=in_specs, out_specs=out_specs, check_vma=False
    )
```

```python
from functools import partial

import jax
import jax.numpy as jnp
from jax import lax
from jax.experimental import pallas as pl
from jax.experimental.pallas import tpu as pltpu
from jax.sharding import PartitionSpec as P

LEARN_RATE = 0.05
WEIGHT_DECAY = 0.1
BETA_ONE = 0.9
BETA_TWO = 0.95
EPSILON = 1e-08

Z_HI, Y, CORES = 2, 4, 2
N_FSDP = Z_HI * Y * CORES
N_GROUP = 16
LEVELS = N_GROUP.bit_length() - 1
ROWS = 160
TOK = 384
WIDTH = 2560
CHUNKS = ((0, 1280), (1280, 1280))
TILE = 1280
DIRECT = (1, -1, 2, 0)
STRIP = 16
SMALL = pl.CostEstimate(flops=1024, bytes_accessed=1024, transcendentals=0)
PARAMS = pltpu.CompilerParams(vmem_limit_bytes=32 * 1024 * 1024)


def held(array):
    return pltpu.with_memory_space_constraint(array, pltpu.HBM)


def fsdp_move(block, move):
    def target(i):
        z, y, c = i // (Y * CORES), (i // CORES) % Y, i % CORES
        z, y, c = move(z, y, c)
        return ((z % Z_HI) * Y + y % Y) * CORES + c % CORES

    return lax.ppermute(block, "fsdp", [(i, target(i)) for i in range(N_FSDP)])


def y_move(block, shift):
    return fsdp_move(block, lambda z, y, c: (z, y + shift, c))


def z_swap(block):
    return fsdp_move(block, lambda z, y, c: (z + 1, y, c))


def core_swap(block):
    return fsdp_move(block, lambda z, y, c: (z, y, c + 1))


def group_move(block, distance):
    return lax.ppermute(
        block, "group", [((i - distance) % N_GROUP, i) for i in range(N_GROUP)]
    )


def turn_kernel(core_ref, x_ref, *refs):
    own_ref, other_ref, turned = refs[-3:]

    def one(j, carry):
        at = pl.multiple_of(j * 256, 256)
        turned[pl.ds(at, 256), :] = x_ref[:, pl.ds(at, 256)].T
        return carry

    lax.fori_loop(0, WIDTH // 256, one, 0)
    core = core_ref[0]

    def give(b, carry):
        for ref, k in ((own_ref, core), (other_ref, 1 - core)):
            start = pl.multiple_of((b * CORES + k) * ROWS, ROWS)
            ref[b] = turned[pl.ds(start, ROWS), :]
        return carry

    lax.fori_loop(0, Z_HI * Y, give, 0)


def turn(core, x, step, after):
    shape = jax.ShapeDtypeStruct((Z_HI * Y, ROWS, TOK), jnp.bfloat16)
    return pl.pallas_call(
        turn_kernel,
        grid_spec=pltpu.PrefetchScalarGridSpec(
            num_scalar_prefetch=1,
            grid=(1,),
            in_specs=[pl.BlockSpec((None, None, TOK, WIDTH), lambda i, s: (step, 0, 0, 0))]
            + [pl.BlockSpec(memory_space=pl.ANY)] * len(after),
            out_specs=[pl.BlockSpec((Z_HI * Y, ROWS, TOK), lambda i, s: (0, 0, 0))] * 2,
            scratch_shapes=[pltpu.VMEM((WIDTH, TOK), jnp.bfloat16)],
        ),
        out_shape=[shape, shape],
        compiler_params=PARAMS,
        cost_estimate=SMALL,
    )(core, held(x), *after)


def products_kernel(adds, layout, terms, tiles, blocks_ref, *refs):
    units = len(adds)
    own, other = refs[:units], refs[units : 2 * units]
    at = 2 * units + 2 * tiles
    y_own, y_other = refs[2 * units : at - tiles], refs[at - tiles : at]
    given = [refs[at + t * tiles : at + (t + 1) * tiles] for t in range(terms)]
    outs = refs[len(refs) - len(layout) :]
    x = jnp.concatenate(
        [jnp.concatenate([a[0], b[0]], axis=1) for a, b in zip(own, other)], axis=0
    )
    total = jnp.concatenate(
        [
            jnp.dot(
                x,
                jnp.concatenate([a[...], b[...]], axis=0),
                preferred_element_type=jnp.float32,
            )
            for a, b in zip(y_own, y_other)
        ],
        axis=1,
    )
    parts = []
    for u, per_unit in enumerate(adds):
        part = total[u * ROWS : (u + 1) * ROWS]
        for term, plane in per_unit:
            more = jnp.concatenate([r[plane] for r in given[term]], axis=1)
            part = part + more.astype(jnp.float32)
        parts.append(part)
    for out, planes in zip(outs, layout):
        for p, u in enumerate(planes):
            out[p] = parts[u].astype(out.dtype)


def products(pair, step, chunk, blocks, adds, terms, layout, dtypes, after=(), hold=False):
    x_own, x_other, y_own, y_other = pair
    if hold:
        y_own, y_other = held(y_own), held(y_other)
    column, width = chunk
    units = len(adds)
    x_specs = [
        pl.BlockSpec((1, ROWS, TOK), lambda j, s, u=u: (s[u], 0, 0)) for u in range(units)
    ]
    tiles = width // TILE
    y_specs = [
        pl.BlockSpec((None, None, TOK, TILE), lambda j, s, t=t: (step, 0, 0, column // TILE + t))
        for t in range(tiles)
    ]

    t_specs = [
        pl.BlockSpec((t.shape[0], ROWS, TILE), lambda j, s, k=first // TILE + k: (0, 0, k))
        for t, first in terms
        for k in range(tiles)
    ]
    outs = [(len(planes), ROWS, width) for planes in layout]
    return pl.pallas_call(
        partial(products_kernel, adds, layout, len(terms), tiles),
        grid_spec=pltpu.PrefetchScalarGridSpec(
            num_scalar_prefetch=1,
            grid=(1,),
            in_specs=x_specs * 2
            + y_specs * 2
            + t_specs
            + [pl.BlockSpec(memory_space=pl.ANY)] * len(after),
            out_specs=[pl.BlockSpec(o, lambda j, s: (0, 0, 0)) for o in outs],
        ),
        out_shape=[jax.ShapeDtypeStruct(o, d) for o, d in zip(outs, dtypes)],
        compiler_params=PARAMS,
        cost_estimate=SMALL,
    )(
        blocks,
        *([x_own] * units),
        *([x_other] * units),
        *([y_own] * tiles),
        *([y_other] * tiles),
        *(t for t, _ in terms for _ in range(tiles)),
        *after,
    )


def strips(work):
    def one(i, carry):
        work(pl.ds(pl.multiple_of(i * STRIP, STRIP), STRIP))
        return carry

    lax.fori_loop(0, ROWS // STRIP, one, 0)


def by_columns(kernel, ins, outs, width, after=(), into=None):
    def spec(array, column, plane=0):
        lead = (None,) * (len(array.shape) - 2)
        return pl.BlockSpec(
            (*lead, ROWS, TILE), lambda j: (*(plane for _ in lead), 0, column // TILE + j)
        )

    shapes = [jax.ShapeDtypeStruct((ROWS, columns), dtype) for columns, _, dtype in outs]
    unread = list(after)
    aliases = {}
    if into is not None:
        aliases = {len(ins) + len(unread): len(outs) - 1}
        unread.append(into)

    def body(*refs):
        used = refs[: len(ins)] + refs[len(ins) + len(unread) :]
        strips(partial(kernel, *used))

    return pl.pallas_call(
        body,
        grid=(width // TILE,),
        in_specs=[spec(*i) for i in ins] + [pl.BlockSpec(memory_space=pl.ANY)] * len(unread),
        out_specs=[spec(shape, o[1]) for shape, o in zip(shapes, outs)],
        out_shape=shapes,
        input_output_aliases=aliases,
        compiler_params=PARAMS,
        cost_estimate=SMALL,
    )(*(i[0] for i in ins), *unread)


def adam(params, first, second, gradient):
    first = BETA_ONE * first + (1.0 - BETA_ONE) * gradient
    second = BETA_TWO * second + (1.0 - BETA_TWO) * gradient * gradient
    updated = params - LEARN_RATE * (first / (jnp.sqrt(second) + EPSILON) + WEIGHT_DECAY * params)
    return first, second, updated.astype(jnp.bfloat16)


def average(own, partner):
    return ((own.astype(jnp.float32) + partner.astype(jnp.float32)) * 0.5).astype(jnp.bfloat16)


def gradient_of(terms, at):
    total = terms[0][at].astype(jnp.float32)
    for term in terms[1:]:
        total = total + term[at].astype(jnp.float32)
    return total


def first_kernel(w, m, v, *rest):
    *terms, new_m, new_v, new_u, at = rest
    f32 = jnp.float32
    new_m[at], new_v[at], new_u[at] = adam(
        w[at].astype(f32), m[at].astype(f32), v[at].astype(f32), gradient_of(terms, at)
    )


def second_kernel(own, partner, m, v, *rest):
    *terms, new_u, new_m, at = rest
    w = average(own[at], partner[at]).astype(jnp.float32)
    new_m[at], _, new_u[at] = adam(w, m[at], v[at], gradient_of(terms, at))


def give_kernel(mine, mine_up, mine_down, other, up, down, total, give, at):
    total[at] = gradient_of((mine, mine_up, mine_down), at)
    give[at] = gradient_of((other, up, down), at).astype(give.dtype)


def average_kernel(own, partner, out, at):
    out[at] = average(own[at], partner[at])


def per_device(x, y, weight, first, second, step_index):
    index = lax.axis_index("fsdp")
    core, at_y, at_z = index % CORES, (index // CORES) % Y, index // (Y * CORES)
    bf16, f32 = jnp.bfloat16, jnp.float32

    def chosen(*pairs):
        rows = [((at_z + dz) % Z_HI) * Y + (at_y + dy) % Y for dy, dz in pairs]
        return jnp.stack(rows).astype(jnp.int32)

    core = core.astype(jnp.int32)[None]
    y_other = core_swap(y)
    last = []
    pairs = []
    for s in range(2):
        x_own, x_give = turn(core, x, s, tuple(last))
        last[:] = [x_own]
        pairs.append((x_own, core_swap(x_give), y, y_other))

    def go(step, chunk, blocks, adds, terms, layout, hold=False):
        outs = products(
            pairs[step],
            step,
            chunk,
            chosen(*blocks),
            adds,
            terms,
            layout,
            (bf16,) * len(layout),
            tuple(last),
            hold,
        )
        last[:] = [outs[0]]
        return outs

    def far(step, chunk):
        up, down = go(step, chunk, ((2, 0), (2, 1)), ((), ()), (), ((0,), (1,)), step == 0)
        return y_move(up, 1), y_move(down, -1)

    def near(step, chunk, arrived):
        up, down, mine, other = go(
            step,
            chunk,
            ((1, 0), (1, 1), (-1, 0), (-1, 1), (0, 0), (0, 1)),
            (((0, 0),), (), (), ((1, 0),), (), ()),
            [(t, chunk[0]) for t in arrived],
            ((0, 1), (2, 3), (4,), (5,)),
        )
        return y_move(up, 1), y_move(down, -1), mine, other

    def follow(kernel, ins, outs, width, into=None):
        results = by_columns(kernel, ins, outs, width, tuple(last), into)
        last[:] = [results[0]]
        return results

    def across(chunk, sums):
        up, down, mine, other = sums
        return follow(
            give_kernel,
            [(mine, 0), (up, 0), (down, 0), (other, 0), (up, 0, 1), (down, 0, 1)],
            [(chunk[1], 0, f32), (chunk[1], 0, bf16)],
            chunk[1],
        )

    def first_step(chunk, total, give):
        column, width = chunk
        return follow(
            first_kernel,
            [(t, column) for t in (weight, first, second)] + [(total, 0), (z_swap(give), 0)],
            [(width, 0, f32), (width, 0, f32), (width, 0, bf16)],
            width,
        )

    def z_first(step, chunk):
        gives = go(
            step, chunk, tuple((dy, 1) for dy in DIRECT), ((),) * Y, (), ((0, 1), (2, 3))
        )
        return [z_swap(give) for give in gives]

    def y_direct(step, chunk, got):
        *sent, mine = go(
            step,
            chunk,
            tuple((dy, 0) for dy in DIRECT),
            tuple(((u // 2, u % 2),) for u in range(Y)),
            [(t, 0) for t in got],
            tuple((u,) for u in range(Y)),
        )
        return [y_move(block, dy) for block, dy in zip(sent, DIRECT)] + [mine]

    a, b = CHUNKS
    far_ab = far(0, (0, WIDTH))
    got_d = z_first(1, b)
    near_a = near(0, a, far_ab)
    near_b = near(0, b, far_ab)
    last.append(got_d[0])
    far_c = far(1, a)
    sums_a = across(a, near_a)
    last.append(got_d[1])
    near_c = near(1, a, far_c)
    sums_b = across(b, near_b)
    terms_d = y_direct(1, b, got_d)
    state_a = first_step(a, *sums_a)
    total_c, give_c = across(a, near_c)
    state_b = first_step(b, *sums_b)
    return lax.switch(
        step_index[0] % LEVELS,
        [partial(ending, level) for level in range(LEVELS)],
        (state_a, state_b),
        total_c,
        give_c,
        terms_d,
    )


def ending(level, states, total_c, give_c, terms_d):
    distances = 1 << level, 1 << ((level + 1) % LEVELS)
    bf16, f32 = jnp.bfloat16, jnp.float32
    terms = [total_c, z_swap(give_c)], terms_d
    partners = [group_move(state[2], distances[0]) for state in states]
    moments, after, boths = None, (), []
    for chunk, state, partner, parts in zip(CHUNKS, states, partners, terms):
        column, width = chunk
        m, v, u = state
        u, moments = by_columns(
            second_kernel,
            [(t, 0) for t in (u, partner, m, v, *parts)],
            [(width, 0, bf16), (WIDTH, column, f32)],
            width,
            after,
            moments,
        )
        after = (u,)
        boths.append((u, group_move(u, distances[1])))
    weights = None
    for (column, width), both in zip(CHUNKS, boths):
        (weights,) = by_columns(
            average_kernel, [(t, 0) for t in both], [(WIDTH, column, bf16)], width, after, weights
        )
        after = ()
    return weights[None], moments[None]


def solution(mesh):
    in_specs = (
        P(None, "group", "fsdp", None),
        P(None, "group", "fsdp", None),
        P("group", "fsdp", None),
        P("group", "fsdp", None),
        P("group", "fsdp", None),
        P(),
    )
    out_specs = (P("group", "fsdp", None), P("group", "fsdp", None))
    return jax.shard_map(
        per_device, mesh=mesh, in_specs=in_specs, out_specs=out_specs, check_vma=False
    )
```

```python
from functools import partial

import jax
import jax.numpy as jnp
from jax import lax
from jax.experimental import pallas as pl
from jax.experimental.pallas import tpu as pltpu
from jax.sharding import PartitionSpec as P

LEARN_RATE = 0.05
WEIGHT_DECAY = 0.1
BETA_ONE = 0.9
BETA_TWO = 0.95
EPSILON = 1e-08

Z_HI, Y, CORES = 2, 4, 2
N_FSDP = Z_HI * Y * CORES
N_GROUP = 16
LEVELS = N_GROUP.bit_length() - 1
ROWS = 160
TOK = 384
WIDTH = 2560
CHUNKS = ((0, 1280), (1280, 1280))
TILE = 1280
STRIP = 16
SMALL = pl.CostEstimate(flops=1024, bytes_accessed=1024, transcendentals=0)
PARAMS = pltpu.CompilerParams(vmem_limit_bytes=32 * 1024 * 1024)


def held(array):
    return pltpu.with_memory_space_constraint(array, pltpu.HBM)


def fsdp_move(block, move):
    def target(i):
        z, y, c = i // (Y * CORES), (i // CORES) % Y, i % CORES
        z, y, c = move(z, y, c)
        return ((z % Z_HI) * Y + y % Y) * CORES + c % CORES

    return lax.ppermute(block, "fsdp", [(i, target(i)) for i in range(N_FSDP)])


def y_move(block, shift):
    return fsdp_move(block, lambda z, y, c: (z, y + shift, c))


def z_swap(block):
    return fsdp_move(block, lambda z, y, c: (z + 1, y, c))


def core_swap(block):
    return fsdp_move(block, lambda z, y, c: (z, y, c + 1))


def group_move(block, distance):
    return lax.ppermute(
        block, "group", [((i - distance) % N_GROUP, i) for i in range(N_GROUP)]
    )


def turn_kernel(core_ref, x_ref, *refs):
    own_ref, other_ref, turned = refs[-3:]

    def one(j, carry):
        at = pl.multiple_of(j * 256, 256)
        turned[pl.ds(at, 256), :] = x_ref[:, pl.ds(at, 256)].T
        return carry

    lax.fori_loop(0, WIDTH // 256, one, 0)
    core = core_ref[0]

    def give(b, carry):
        for ref, k in ((own_ref, core), (other_ref, 1 - core)):
            start = pl.multiple_of((b * CORES + k) * ROWS, ROWS)
            ref[b] = turned[pl.ds(start, ROWS), :]
        return carry

    lax.fori_loop(0, Z_HI * Y, give, 0)


def turn(core, x, step, after):
    shape = jax.ShapeDtypeStruct((Z_HI * Y, ROWS, TOK), jnp.bfloat16)
    return pl.pallas_call(
        turn_kernel,
        grid_spec=pltpu.PrefetchScalarGridSpec(
            num_scalar_prefetch=1,
            grid=(1,),
            in_specs=[pl.BlockSpec((None, None, TOK, WIDTH), lambda i, s: (step, 0, 0, 0))]
            + [pl.BlockSpec(memory_space=pl.ANY)] * len(after),
            out_specs=[pl.BlockSpec((Z_HI * Y, ROWS, TOK), lambda i, s: (0, 0, 0))] * 2,
            scratch_shapes=[pltpu.VMEM((WIDTH, TOK), jnp.bfloat16)],
        ),
        out_shape=[shape, shape],
        compiler_params=PARAMS,
        cost_estimate=SMALL,
    )(core, held(x), *after)


def products_kernel(adds, layout, terms, tiles, blocks_ref, *refs):
    units = len(adds)
    own, other = refs[:units], refs[units : 2 * units]
    at = 2 * units + 2 * tiles
    y_own, y_other = refs[2 * units : at - tiles], refs[at - tiles : at]
    given = [refs[at + t * tiles : at + (t + 1) * tiles] for t in range(terms)]
    outs = refs[len(refs) - len(layout) :]
    x = jnp.concatenate(
        [jnp.concatenate([a[0], b[0]], axis=1) for a, b in zip(own, other)], axis=0
    )
    total = jnp.concatenate(
        [
            jnp.dot(
                x,
                jnp.concatenate([a[...], b[...]], axis=0),
                preferred_element_type=jnp.float32,
            )
            for a, b in zip(y_own, y_other)
        ],
        axis=1,
    )
    parts = []
    for u, per_unit in enumerate(adds):
        part = total[u * ROWS : (u + 1) * ROWS]
        for term, plane in per_unit:
            more = jnp.concatenate([r[plane] for r in given[term]], axis=1)
            part = part + more.astype(jnp.float32)
        parts.append(part)
    for out, planes in zip(outs, layout):
        for p, u in enumerate(planes):
            out[p] = parts[u].astype(out.dtype)


def products(pair, step, chunk, blocks, adds, terms, layout, dtypes, after=(), hold=False):
    x_own, x_other, y_own, y_other = pair
    if hold:
        y_own, y_other = held(y_own), held(y_other)
    column, width = chunk
    units = len(adds)
    x_specs = [
        pl.BlockSpec((1, ROWS, TOK), lambda j, s, u=u: (s[u], 0, 0)) for u in range(units)
    ]
    tiles = width // TILE
    y_specs = [
        pl.BlockSpec((None, None, TOK, TILE), lambda j, s, t=t: (step, 0, 0, column // TILE + t))
        for t in range(tiles)
    ]

    t_specs = [
        pl.BlockSpec((t.shape[0], ROWS, TILE), lambda j, s, k=first // TILE + k: (0, 0, k))
        for t, first in terms
        for k in range(tiles)
    ]
    outs = [(len(planes), ROWS, width) for planes in layout]
    return pl.pallas_call(
        partial(products_kernel, adds, layout, len(terms), tiles),
        grid_spec=pltpu.PrefetchScalarGridSpec(
            num_scalar_prefetch=1,
            grid=(1,),
            in_specs=x_specs * 2
            + y_specs * 2
            + t_specs
            + [pl.BlockSpec(memory_space=pl.ANY)] * len(after),
            out_specs=[pl.BlockSpec(o, lambda j, s: (0, 0, 0)) for o in outs],
        ),
        out_shape=[jax.ShapeDtypeStruct(o, d) for o, d in zip(outs, dtypes)],
        compiler_params=PARAMS,
        cost_estimate=SMALL,
    )(
        blocks,
        *([x_own] * units),
        *([x_other] * units),
        *([y_own] * tiles),
        *([y_other] * tiles),
        *(t for t, _ in terms for _ in range(tiles)),
        *after,
    )


def strips(work):
    def one(i, carry):
        work(pl.ds(pl.multiple_of(i * STRIP, STRIP), STRIP))
        return carry

    lax.fori_loop(0, ROWS // STRIP, one, 0)


def by_columns(kernel, ins, outs, width, after=(), into=None):
    def spec(array, column, plane=0):
        lead = (None,) * (len(array.shape) - 2)
        return pl.BlockSpec(
            (*lead, ROWS, TILE), lambda j: (*(plane for _ in lead), 0, column // TILE + j)
        )

    shapes = [jax.ShapeDtypeStruct((ROWS, columns), dtype) for columns, _, dtype in outs]
    unread = list(after)
    aliases = {}
    if into is not None:
        aliases = {len(ins) + len(unread): len(outs) - 1}
        unread.append(into)

    def body(*refs):
        used = refs[: len(ins)] + refs[len(ins) + len(unread) :]
        strips(partial(kernel, *used))

    return pl.pallas_call(
        body,
        grid=(width // TILE,),
        in_specs=[spec(*i) for i in ins] + [pl.BlockSpec(memory_space=pl.ANY)] * len(unread),
        out_specs=[spec(shape, o[1]) for shape, o in zip(shapes, outs)],
        out_shape=shapes,
        input_output_aliases=aliases,
        compiler_params=PARAMS,
        cost_estimate=SMALL,
    )(*(i[0] for i in ins), *unread)


def adam(params, first, second, gradient):
    first = BETA_ONE * first + (1.0 - BETA_ONE) * gradient
    second = BETA_TWO * second + (1.0 - BETA_TWO) * gradient * gradient
    updated = params - LEARN_RATE * (first / (jnp.sqrt(second) + EPSILON) + WEIGHT_DECAY * params)
    return first, second, updated.astype(jnp.bfloat16)


def average(own, partner):
    return ((own.astype(jnp.float32) + partner.astype(jnp.float32)) * 0.5).astype(jnp.bfloat16)


def gradient_of(terms, at):
    total = terms[0][at].astype(jnp.float32)
    for term in terms[1:]:
        total = total + term[at].astype(jnp.float32)
    return total


def first_kernel(w, m, v, *rest):
    *terms, new_m, new_v, new_u, at = rest
    f32 = jnp.float32
    new_m[at], new_v[at], new_u[at] = adam(
        w[at].astype(f32), m[at].astype(f32), v[at].astype(f32), gradient_of(terms, at)
    )


def second_kernel(own, partner, m, v, *rest):
    *terms, new_u, new_m, at = rest
    w = average(own[at], partner[at]).astype(jnp.float32)
    new_m[at], _, new_u[at] = adam(w, m[at], v[at], gradient_of(terms, at))


def give_kernel(mine, mine_up, mine_down, other, up, down, total, give, at):
    total[at] = gradient_of((mine, mine_up, mine_down), at)
    give[at] = gradient_of((other, up, down), at).astype(give.dtype)


def average_kernel(own, partner, out, at):
    out[at] = average(own[at], partner[at])


def per_device(x, y, weight, first, second, step_index):
    index = lax.axis_index("fsdp")
    core, at_y, at_z = index % CORES, (index // CORES) % Y, index // (Y * CORES)
    bf16, f32 = jnp.bfloat16, jnp.float32

    def chosen(*pairs):
        rows = [((at_z + dz) % Z_HI) * Y + (at_y + dy) % Y for dy, dz in pairs]
        return jnp.stack(rows).astype(jnp.int32)

    core = core.astype(jnp.int32)[None]
    y_other = core_swap(y)
    last = []
    pairs = []
    for s in range(2):
        x_own, x_give = turn(core, x, s, tuple(last))
        last[:] = [x_own]
        pairs.append((x_own, core_swap(x_give), y, y_other))

    def go(step, chunk, blocks, adds, terms, layout, hold=False):
        outs = products(
            pairs[step],
            step,
            chunk,
            chosen(*blocks),
            adds,
            terms,
            layout,
            (bf16,) * len(layout),
            tuple(last),
            hold,
        )
        last[:] = [outs[0]]
        return outs

    def far(step, chunk):
        up, down = go(step, chunk, ((2, 0), (2, 1)), ((), ()), (), ((0,), (1,)), step == 0)
        return y_move(up, 1), y_move(down, -1)

    def near(step, chunk, arrived):
        up, down, mine, other = go(
            step,
            chunk,
            ((1, 0), (1, 1), (-1, 0), (-1, 1), (0, 0), (0, 1)),
            (((0, 0),), (), (), ((1, 0),), (), ()),
            [(t, chunk[0]) for t in arrived],
            ((0, 1), (2, 3), (4,), (5,)),
        )
        return up, down, mine, other

    def sent(up, down, mine, other):
        return y_move(up, 1), y_move(down, -1), mine, other

    def follow(kernel, ins, outs, width, into=None):
        results = by_columns(kernel, ins, outs, width, tuple(last), into)
        last[:] = [results[0]]
        return results

    def across(chunk, sums):
        total, give = give_block(sums, chunk[1], tuple(last))
        last[:] = [total]
        return total, give

    def first_step(chunk, total, got):
        column, width = chunk
        return follow(
            first_kernel,
            [(t, column) for t in (weight, first, second)] + [(total, 0), (got, 0)],
            [(width, 0, f32), (width, 0, f32), (width, 0, bf16)],
            width,
        )

    a, b = CHUNKS
    far_ab = far(0, (0, WIDTH))
    near_a = sent(*near(0, a, far_ab))
    far_cd = far(1, (0, WIDTH))
    total_a, give_a = across(a, near_a)
    sums_a = total_a, z_swap(give_a)
    near_b = sent(*near(0, b, far_ab))
    near_c = sent(*near(1, a, far_cd))
    last.append(sums_a[1])
    total_b, give_b = across(b, near_b)
    sums_b = total_b, z_swap(give_b)
    state_a = first_step(a, *sums_a)
    near_d = near(1, b, far_cd)
    total_c, give_c = across(a, near_c)
    state_b = first_step(b, *sums_b)
    return lax.switch(
        step_index[0] % LEVELS,
        [partial(ending, level) for level in range(LEVELS)],
        (state_a, state_b),
        total_c,
        give_c,
        near_d,
    )


def give_block(sums, width, after):
    up, down, mine, other = sums
    return by_columns(
        give_kernel,
        [(mine, 0), (up, 0), (down, 0), (other, 0), (up, 0, 1), (down, 0, 1)],
        [(width, 0, jnp.float32), (width, 0, jnp.bfloat16)],
        width,
        after,
    )


def ending(level, states, total_c, give_c, near_d):
    distances = 1 << level, 1 << ((level + 1) % LEVELS)
    bf16, f32 = jnp.bfloat16, jnp.float32
    up, down, mine, other = near_d
    near_d = y_move(up, 1), y_move(down, -1), mine, other
    got_c = z_swap(give_c)
    partners = [group_move(state[2], distances[0]) for state in states]
    total_d, give_d = give_block(near_d, CHUNKS[1][1], ())
    terms = (total_c, got_c), (total_d, z_swap(give_d))
    moments, after, boths = None, (total_d,), []
    for chunk, state, partner, parts in zip(CHUNKS, states, partners, terms):
        column, width = chunk
        m, v, u = state
        u, moments = by_columns(
            second_kernel,
            [(t, 0) for t in (u, partner, m, v, *parts)],
            [(width, 0, bf16), (WIDTH, column, f32)],
            width,
            after,
            moments,
        )
        after = (u,)
        boths.append((u, group_move(u, distances[1])))
    weights = None
    for (column, width), both in zip(CHUNKS, boths):
        (weights,) = by_columns(
            average_kernel, [(t, 0) for t in both], [(WIDTH, column, bf16)], width, after, weights
        )
        after = ()
    return weights[None], moments[None]


def solution(mesh):
    in_specs = (
        P(None, "group", "fsdp", None),
        P(None, "group", "fsdp", None),
        P("group", "fsdp", None),
        P("group", "fsdp", None),
        P("group", "fsdp", None),
        P(),
    )
    out_specs = (P("group", "fsdp", None), P("group", "fsdp", None))
    return jax.shard_map(
        per_device, mesh=mesh, in_specs=in_specs, out_specs=out_specs, check_vma=False
    )
```

```python
from functools import partial

import jax
import jax.numpy as jnp
from jax import lax
from jax.experimental import pallas as pl
from jax.experimental.pallas import tpu as pltpu
from jax.sharding import PartitionSpec as P

LEARN_RATE = 0.05
WEIGHT_DECAY = 0.1
BETA_ONE = 0.9
BETA_TWO = 0.95
EPSILON = 1e-08

Z_HI, Y, CORES = 2, 4, 2
N_FSDP = Z_HI * Y * CORES
N_GROUP = 16
LEVELS = N_GROUP.bit_length() - 1
ROWS = 160
TOK = 384
WIDTH = 2560
CHUNKS = ((0, 1280), (1280, 1280))
TILE = 1280
STRIP = 16
SMALL = pl.CostEstimate(flops=1024, bytes_accessed=1024, transcendentals=0)
PARAMS = pltpu.CompilerParams(vmem_limit_bytes=32 * 1024 * 1024)


def held(array):
    return pltpu.with_memory_space_constraint(array, pltpu.HBM)


def fsdp_move(block, move):
    def target(i):
        z, y, c = i // (Y * CORES), (i // CORES) % Y, i % CORES
        z, y, c = move(z, y, c)
        return ((z % Z_HI) * Y + y % Y) * CORES + c % CORES

    return lax.ppermute(block, "fsdp", [(i, target(i)) for i in range(N_FSDP)])


def y_move(block, shift):
    return fsdp_move(block, lambda z, y, c: (z, y + shift, c))


def z_swap(block):
    return fsdp_move(block, lambda z, y, c: (z + 1, y, c))


def core_swap(block):
    return fsdp_move(block, lambda z, y, c: (z, y, c + 1))


def group_move(block, distance):
    return lax.ppermute(
        block, "group", [((i - distance) % N_GROUP, i) for i in range(N_GROUP)]
    )


def turn_kernel(core_ref, x_ref, *refs):
    own_ref, other_ref, turned = refs[-3:]

    def one(j, carry):
        at = pl.multiple_of(j * 256, 256)
        turned[pl.ds(at, 256), :] = x_ref[:, pl.ds(at, 256)].T
        return carry

    lax.fori_loop(0, WIDTH // 256, one, 0)
    core = core_ref[0]

    def give(b, carry):
        for ref, k in ((own_ref, core), (other_ref, 1 - core)):
            start = pl.multiple_of((b * CORES + k) * ROWS, ROWS)
            ref[b] = turned[pl.ds(start, ROWS), :]
        return carry

    lax.fori_loop(0, Z_HI * Y, give, 0)


def turn(core, x, step, after):
    shape = jax.ShapeDtypeStruct((Z_HI * Y, ROWS, TOK), jnp.bfloat16)
    return pl.pallas_call(
        turn_kernel,
        grid_spec=pltpu.PrefetchScalarGridSpec(
            num_scalar_prefetch=1,
            grid=(1,),
            in_specs=[pl.BlockSpec((None, None, TOK, WIDTH), lambda i, s: (step, 0, 0, 0))]
            + [pl.BlockSpec(memory_space=pl.ANY)] * len(after),
            out_specs=[pl.BlockSpec((Z_HI * Y, ROWS, TOK), lambda i, s: (0, 0, 0))] * 2,
            scratch_shapes=[pltpu.VMEM((WIDTH, TOK), jnp.bfloat16)],
        ),
        out_shape=[shape, shape],
        compiler_params=PARAMS,
        cost_estimate=SMALL,
    )(core, held(x), *after)


def products_kernel(adds, layout, terms, tiles, blocks_ref, *refs):
    units = len(adds)
    own, other = refs[:units], refs[units : 2 * units]
    at = 2 * units + 2 * tiles
    y_own, y_other = refs[2 * units : at - tiles], refs[at - tiles : at]
    given = [refs[at + t * tiles : at + (t + 1) * tiles] for t in range(terms)]
    outs = refs[len(refs) - len(layout) :]
    x = jnp.concatenate(
        [jnp.concatenate([a[0], b[0]], axis=1) for a, b in zip(own, other)], axis=0
    )
    total = jnp.concatenate(
        [
            jnp.dot(
                x,
                jnp.concatenate([a[...], b[...]], axis=0),
                preferred_element_type=jnp.float32,
            )
            for a, b in zip(y_own, y_other)
        ],
        axis=1,
    )
    parts = []
    for u, per_unit in enumerate(adds):
        part = total[u * ROWS : (u + 1) * ROWS]
        for term, plane in per_unit:
            more = jnp.concatenate([r[plane] for r in given[term]], axis=1)
            part = part + more.astype(jnp.float32)
        parts.append(part)
    for out, planes in zip(outs, layout):
        for p, u in enumerate(planes):
            out[p] = parts[u].astype(out.dtype)


def products(pair, step, chunk, blocks, adds, terms, layout, dtypes, after=(), hold=False):
    x_own, x_other, y_own, y_other = pair
    if hold:
        y_own, y_other = held(y_own), held(y_other)
    column, width = chunk
    units = len(adds)
    x_specs = [
        pl.BlockSpec((1, ROWS, TOK), lambda j, s, u=u: (s[u], 0, 0)) for u in range(units)
    ]
    tiles = width // TILE
    y_specs = [
        pl.BlockSpec((None, None, TOK, TILE), lambda j, s, t=t: (step, 0, 0, column // TILE + t))
        for t in range(tiles)
    ]

    t_specs = [
        pl.BlockSpec((t.shape[0], ROWS, TILE), lambda j, s, k=first // TILE + k: (0, 0, k))
        for t, first in terms
        for k in range(tiles)
    ]
    outs = [(len(planes), ROWS, width) for planes in layout]
    return pl.pallas_call(
        partial(products_kernel, adds, layout, len(terms), tiles),
        grid_spec=pltpu.PrefetchScalarGridSpec(
            num_scalar_prefetch=1,
            grid=(1,),
            in_specs=x_specs * 2
            + y_specs * 2
            + t_specs
            + [pl.BlockSpec(memory_space=pl.ANY)] * len(after),
            out_specs=[pl.BlockSpec(o, lambda j, s: (0, 0, 0)) for o in outs],
        ),
        out_shape=[jax.ShapeDtypeStruct(o, d) for o, d in zip(outs, dtypes)],
        compiler_params=PARAMS,
        cost_estimate=SMALL,
    )(
        blocks,
        *([x_own] * units),
        *([x_other] * units),
        *([y_own] * tiles),
        *([y_other] * tiles),
        *(t for t, _ in terms for _ in range(tiles)),
        *after,
    )


def strips(work):
    def one(i, carry):
        row = pl.multiple_of((i // 2) * STRIP, STRIP)
        column = pl.multiple_of((i % 2) * (TILE // 2), TILE // 2)
        work((pl.ds(row, STRIP), pl.ds(column, TILE // 2)))
        return carry

    lax.fori_loop(0, 2 * (ROWS // STRIP), one, 0)


def by_columns(kernel, ins, outs, width, after=(), into=None):
    def spec(array, column, plane=0):
        lead = (None,) * (len(array.shape) - 2)
        return pl.BlockSpec(
            (*lead, ROWS, TILE), lambda j: (*(plane for _ in lead), 0, column // TILE + j)
        )

    shapes = [jax.ShapeDtypeStruct((ROWS, columns), dtype) for columns, _, dtype in outs]
    unread = list(after)
    aliases = {}
    if into is not None:
        aliases = {len(ins) + len(unread): len(outs) - 1}
        unread.append(into)

    def body(*refs):
        used = refs[: len(ins)] + refs[len(ins) + len(unread) :]
        strips(partial(kernel, *used))

    return pl.pallas_call(
        body,
        grid=(width // TILE,),
        in_specs=[spec(*i) for i in ins] + [pl.BlockSpec(memory_space=pl.ANY)] * len(unread),
        out_specs=[spec(shape, o[1]) for shape, o in zip(shapes, outs)],
        out_shape=shapes,
        input_output_aliases=aliases,
        compiler_params=PARAMS,
        cost_estimate=SMALL,
    )(*(i[0] for i in ins), *unread)


def adam(params, first, second, gradient):
    first = BETA_ONE * first + (1.0 - BETA_ONE) * gradient
    second = BETA_TWO * second + (1.0 - BETA_TWO) * gradient * gradient
    updated = params - LEARN_RATE * (first / (jnp.sqrt(second) + EPSILON) + WEIGHT_DECAY * params)
    return first, second, updated.astype(jnp.bfloat16)


def average(own, partner):
    return ((own.astype(jnp.float32) + partner.astype(jnp.float32)) * 0.5).astype(jnp.bfloat16)


def gradient_of(terms, at):
    total = terms[0][at].astype(jnp.float32)
    for term in terms[1:]:
        total = total + term[at].astype(jnp.float32)
    return total


def first_kernel(w, m, v, *rest):
    *terms, new_m, new_v, new_u, at = rest
    f32 = jnp.float32
    new_m[at], new_v[at], new_u[at] = adam(
        w[at].astype(f32), m[at].astype(f32), v[at].astype(f32), gradient_of(terms, at)
    )


def second_kernel(own, partner, m, v, *rest):
    *terms, new_u, new_m, at = rest
    w = average(own[at], partner[at]).astype(jnp.float32)
    new_m[at], _, new_u[at] = adam(w, m[at], v[at], gradient_of(terms, at))


def give_kernel(mine, mine_up, mine_down, other, up, down, total, give, at):
    total[at] = gradient_of((mine, mine_up, mine_down), at)
    give[at] = gradient_of((other, up, down), at).astype(give.dtype)


def average_kernel(own, partner, out, at):
    out[at] = average(own[at], partner[at])


def per_device(x, y, weight, first, second, step_index):
    index = lax.axis_index("fsdp")
    core, at_y, at_z = index % CORES, (index // CORES) % Y, index // (Y * CORES)
    bf16, f32 = jnp.bfloat16, jnp.float32

    def chosen(*pairs):
        rows = [((at_z + dz) % Z_HI) * Y + (at_y + dy) % Y for dy, dz in pairs]
        return jnp.stack(rows).astype(jnp.int32)

    core = core.astype(jnp.int32)[None]
    y_other = core_swap(y)
    last = []
    pairs = []
    for s in range(2):
        x_own, x_give = turn(core, x, s, tuple(last))
        last[:] = [x_own]
        pairs.append((x_own, core_swap(x_give), y, y_other))

    def go(step, chunk, blocks, adds, terms, layout, hold=False):
        outs = products(
            pairs[step],
            step,
            chunk,
            chosen(*blocks),
            adds,
            terms,
            layout,
            (bf16,) * len(layout),
            tuple(last),
            hold,
        )
        last[:] = [outs[0]]
        return outs

    def far(step, chunk):
        up, down = go(step, chunk, ((2, 0), (2, 1)), ((), ()), (), ((0,), (1,)), step == 0)
        return y_move(up, 1), y_move(down, -1)

    def near(step, chunk, arrived):
        up, down, mine, other = go(
            step,
            chunk,
            ((1, 0), (1, 1), (-1, 0), (-1, 1), (0, 0), (0, 1)),
            (((0, 0),), (), (), ((1, 0),), (), ()),
            [(t, chunk[0]) for t in arrived],
            ((0, 1), (2, 3), (4,), (5,)),
        )
        return y_move(up, 1), y_move(down, -1), mine, other

    def follow(kernel, ins, outs, width, into=None):
        results = by_columns(kernel, ins, outs, width, tuple(last), into)
        last[:] = [results[0]]
        return results

    def across(chunk, sums):
        up, down, mine, other = sums
        return follow(
            give_kernel,
            [(mine, 0), (up, 0), (down, 0), (other, 0), (up, 0, 1), (down, 0, 1)],
            [(chunk[1], 0, f32), (chunk[1], 0, bf16)],
            chunk[1],
        )

    def first_step(chunk, total, give):
        column, width = chunk
        return follow(
            first_kernel,
            [(t, column) for t in (weight, first, second)] + [(total, 0), (z_swap(give), 0)],
            [(width, 0, f32), (width, 0, f32), (width, 0, bf16)],
            width,
        )

    a, b = CHUNKS
    far_ab = far(0, (0, WIDTH))
    near_a = near(0, a, far_ab)
    far_cd = far(1, (0, WIDTH))
    sums_a = across(a, near_a)
    near_b = near(0, b, far_ab)
    near_c = near(1, a, far_cd)
    sums_b = across(b, near_b)
    state_a = first_step(a, *sums_a)
    near_d = near(1, b, far_cd)
    state_b = first_step(b, *sums_b)
    total_c, give_c = across(a, near_c)
    total_d, give_d = across(b, near_d)
    return lax.switch(
        step_index[0] % LEVELS,
        [partial(ending, level) for level in range(LEVELS)],
        state_a,
        state_b,
        total_c,
        total_d,
        z_swap(give_c),
        give_d,
    )


def ending(level, state_a, state_b, total_c, total_d, got_c, give_d):
    distances = 1 << level, 1 << ((level + 1) % LEVELS)
    bf16, f32 = jnp.bfloat16, jnp.float32
    partners = [group_move(state[2], distances[0]) for state in (state_a, state_b)]
    gots = got_c, z_swap(give_d)
    moments, after, boths = None, (), []
    for chunk, state, partner, total, got in zip(
        CHUNKS, (state_a, state_b), partners, (total_c, total_d), gots
    ):
        column, width = chunk
        m, v, u = state
        u, moments = by_columns(
            second_kernel,
            [(t, 0) for t in (u, partner, m, v, total, got)],
            [(width, 0, bf16), (WIDTH, column, f32)],
            width,
            after,
            moments,
        )
        after = (u,)
        boths.append((u, group_move(u, distances[1])))
    weights = None
    for (column, width), both in zip(CHUNKS, boths):
        (weights,) = by_columns(
            average_kernel, [(t, 0) for t in both], [(WIDTH, column, bf16)], width, after, weights
        )
        after = ()
    return weights[None], moments[None]


def solution(mesh):
    in_specs = (
        P(None, "group", "fsdp", None),
        P(None, "group", "fsdp", None),
        P("group", "fsdp", None),
        P("group", "fsdp", None),
        P("group", "fsdp", None),
        P(),
    )
    out_specs = (P("group", "fsdp", None), P("group", "fsdp", None))
    return jax.shard_map(
        per_device, mesh=mesh, in_specs=in_specs, out_specs=out_specs, check_vma=False
    )
```

```python
from functools import partial

import jax
import jax.numpy as jnp
from jax import lax
from jax.experimental import pallas as pl
from jax.experimental.pallas import tpu as pltpu
from jax.sharding import PartitionSpec as P

LEARN_RATE = 0.05
WEIGHT_DECAY = 0.1
BETA_ONE = 0.9
BETA_TWO = 0.95
EPSILON = 1e-08

Z_HI, Y, CORES = 2, 4, 2
N_FSDP = Z_HI * Y * CORES
N_GROUP = 16
LEVELS = N_GROUP.bit_length() - 1
ROWS = 160
TOK = 384
WIDTH = 2560
CHUNKS = ((0, 1280), (1280, 1280))
TILE = 1280
STRIP = 16
SMALL = pl.CostEstimate(flops=1024, bytes_accessed=1024, transcendentals=0)
PARAMS = pltpu.CompilerParams(vmem_limit_bytes=32 * 1024 * 1024)


def held(array):
    return pltpu.with_memory_space_constraint(array, pltpu.HBM)


def fsdp_move(block, move):
    def target(i):
        z, y, c = i // (Y * CORES), (i // CORES) % Y, i % CORES
        z, y, c = move(z, y, c)
        return ((z % Z_HI) * Y + y % Y) * CORES + c % CORES

    return lax.ppermute(block, "fsdp", [(i, target(i)) for i in range(N_FSDP)])


def y_move(block, shift):
    return fsdp_move(block, lambda z, y, c: (z, y + shift, c))


def z_swap(block):
    return fsdp_move(block, lambda z, y, c: (z + 1, y, c))


def core_swap(block):
    return fsdp_move(block, lambda z, y, c: (z, y, c + 1))


def group_move(block, distance):
    return lax.ppermute(
        block, "group", [((i - distance) % N_GROUP, i) for i in range(N_GROUP)]
    )


def turn_kernel(core_ref, x_ref, *refs):
    own_ref, other_ref, turned = refs[-3:]

    def one(j, carry):
        at = pl.multiple_of(j * 256, 256)
        turned[pl.ds(at, 256), :] = x_ref[:, pl.ds(at, 256)].T
        return carry

    lax.fori_loop(0, WIDTH // 256, one, 0)
    core = core_ref[0]

    def give(b, carry):
        for ref, k in ((own_ref, core), (other_ref, 1 - core)):
            start = pl.multiple_of((b * CORES + k) * ROWS, ROWS)
            ref[b] = turned[pl.ds(start, ROWS), :]
        return carry

    lax.fori_loop(0, Z_HI * Y, give, 0)


def turn(core, x, step, after):
    shape = jax.ShapeDtypeStruct((Z_HI * Y, ROWS, TOK), jnp.bfloat16)
    return pl.pallas_call(
        turn_kernel,
        grid_spec=pltpu.PrefetchScalarGridSpec(
            num_scalar_prefetch=1,
            grid=(1,),
            in_specs=[pl.BlockSpec((None, None, TOK, WIDTH), lambda i, s: (step, 0, 0, 0))]
            + [pl.BlockSpec(memory_space=pl.ANY)] * len(after),
            out_specs=[pl.BlockSpec((Z_HI * Y, ROWS, TOK), lambda i, s: (0, 0, 0))] * 2,
            scratch_shapes=[pltpu.VMEM((WIDTH, TOK), jnp.bfloat16)],
        ),
        out_shape=[shape, shape],
        compiler_params=PARAMS,
        cost_estimate=SMALL,
    )(core, held(x), *after)


def products_kernel(adds, layout, terms, tiles, blocks_ref, *refs):
    units = len(adds)
    own, other = refs[:units], refs[units : 2 * units]
    at = 2 * units + 2 * tiles
    y_own, y_other = refs[2 * units : at - tiles], refs[at - tiles : at]
    given = [refs[at + t * tiles : at + (t + 1) * tiles] for t in range(terms)]
    outs = refs[len(refs) - len(layout) :]
    x = jnp.concatenate(
        [jnp.concatenate([a[0], b[0]], axis=1) for a, b in zip(own, other)], axis=0
    )
    total = jnp.concatenate(
        [
            jnp.dot(
                x,
                jnp.concatenate([a[...], b[...]], axis=0),
                preferred_element_type=jnp.float32,
            )
            for a, b in zip(y_own, y_other)
        ],
        axis=1,
    )
    parts = []
    for u, per_unit in enumerate(adds):
        part = total[u * ROWS : (u + 1) * ROWS]
        for term, plane in per_unit:
            more = jnp.concatenate([r[plane] for r in given[term]], axis=1)
            part = part + more.astype(jnp.float32)
        parts.append(part)
    for out, planes in zip(outs, layout):
        for p, u in enumerate(planes):
            out[p] = parts[u].astype(out.dtype)


def products(pair, step, chunk, blocks, adds, terms, layout, dtypes, after=(), hold=False):
    x_own, x_other, y_own, y_other = pair
    if hold:
        y_own, y_other = held(y_own), held(y_other)
    column, width = chunk
    units = len(adds)
    x_specs = [
        pl.BlockSpec((1, ROWS, TOK), lambda j, s, u=u: (s[u], 0, 0)) for u in range(units)
    ]
    tiles = width // TILE
    y_specs = [
        pl.BlockSpec((None, None, TOK, TILE), lambda j, s, t=t: (step, 0, 0, column // TILE + t))
        for t in range(tiles)
    ]

    t_specs = [
        pl.BlockSpec((t.shape[0], ROWS, TILE), lambda j, s, k=first // TILE + k: (0, 0, k))
        for t, first in terms
        for k in range(tiles)
    ]
    outs = [(len(planes), ROWS, width) for planes in layout]
    return pl.pallas_call(
        partial(products_kernel, adds, layout, len(terms), tiles),
        grid_spec=pltpu.PrefetchScalarGridSpec(
            num_scalar_prefetch=1,
            grid=(1,),
            in_specs=x_specs * 2
            + y_specs * 2
            + t_specs
            + [pl.BlockSpec(memory_space=pl.ANY)] * len(after),
            out_specs=[pl.BlockSpec(o, lambda j, s: (0, 0, 0)) for o in outs],
        ),
        out_shape=[jax.ShapeDtypeStruct(o, d) for o, d in zip(outs, dtypes)],
        compiler_params=PARAMS,
        cost_estimate=SMALL,
    )(
        blocks,
        *([x_own] * units),
        *([x_other] * units),
        *([y_own] * tiles),
        *([y_other] * tiles),
        *(t for t, _ in terms for _ in range(tiles)),
        *after,
    )


def strips(work):
    def one(i, carry):
        work(pl.ds(pl.multiple_of(i * STRIP, STRIP), STRIP))
        return carry

    lax.fori_loop(0, ROWS // STRIP, one, 0)


def by_columns(kernel, ins, outs, width, after=(), into=None):
    def spec(array, column, plane=0):
        lead = (None,) * (len(array.shape) - 2)
        return pl.BlockSpec(
            (*lead, ROWS, TILE), lambda j: (*(plane for _ in lead), 0, column // TILE + j)
        )

    shapes = [jax.ShapeDtypeStruct((ROWS, columns), dtype) for columns, _, dtype in outs]
    unread = list(after)
    aliases = {}
    if into is not None:
        aliases = {len(ins) + len(unread): len(outs) - 1}
        unread.append(into)

    def body(*refs):
        used = refs[: len(ins)] + refs[len(ins) + len(unread) :]
        strips(partial(kernel, *used))

    return pl.pallas_call(
        body,
        grid=(width // TILE,),
        in_specs=[spec(*i) for i in ins] + [pl.BlockSpec(memory_space=pl.ANY)] * len(unread),
        out_specs=[spec(shape, o[1]) for shape, o in zip(shapes, outs)],
        out_shape=shapes,
        input_output_aliases=aliases,
        compiler_params=PARAMS,
        cost_estimate=SMALL,
    )(*(i[0] for i in ins), *unread)


def adam(params, first, second, gradient):
    first = BETA_ONE * first + (1.0 - BETA_ONE) * gradient
    second = BETA_TWO * second + (1.0 - BETA_TWO) * gradient * gradient
    updated = params - LEARN_RATE * (first / (jnp.sqrt(second) + EPSILON) + WEIGHT_DECAY * params)
    return first, second, updated.astype(jnp.bfloat16)


def average(own, partner):
    return ((own.astype(jnp.float32) + partner.astype(jnp.float32)) * 0.5).astype(jnp.bfloat16)


def gradient_of(terms, at):
    total = terms[0][at].astype(jnp.float32)
    for term in terms[1:]:
        total = total + term[at].astype(jnp.float32)
    return total


def first_kernel(w, m, v, *rest):
    *terms, new_m, new_v, new_u, at = rest
    f32 = jnp.float32
    new_m[at], new_v[at], new_u[at] = adam(
        w[at].astype(f32), m[at].astype(f32), v[at].astype(f32), gradient_of(terms, at)
    )


def second_kernel(own, partner, m, v, *rest):
    *terms, new_u, new_m, at = rest
    w = average(own[at], partner[at]).astype(jnp.float32)
    new_m[at], _, new_u[at] = adam(w, m[at], v[at], gradient_of(terms, at))


def give_kernel(mine, mine_up, mine_down, other, up, down, total, give, at):
    total[at] = gradient_of((mine, mine_up, mine_down), at)
    give[at] = gradient_of((other, up, down), at).astype(give.dtype)


def average_kernel(own, partner, out, at):
    out[at] = average(own[at], partner[at])


def per_device(x, y, weight, first, second, step_index):
    index = lax.axis_index("fsdp")
    core, at_y, at_z = index % CORES, (index // CORES) % Y, index // (Y * CORES)
    bf16, f32 = jnp.bfloat16, jnp.float32

    def chosen(*pairs):
        rows = [((at_z + dz) % Z_HI) * Y + (at_y + dy) % Y for dy, dz in pairs]
        return jnp.stack(rows).astype(jnp.int32)

    core = core.astype(jnp.int32)[None]
    y_other = core_swap(y)
    last = []
    pairs = []
    for s in range(2):
        x_own, x_give = turn(core, x, s, tuple(last))
        last[:] = [x_own]
        pairs.append((x_own, core_swap(x_give), y, y_other))

    def go(step, chunk, blocks, adds, terms, layout, hold=False):
        outs = products(
            pairs[step],
            step,
            chunk,
            chosen(*blocks),
            adds,
            terms,
            layout,
            (bf16,) * len(layout),
            tuple(last),
            hold,
        )
        last[:] = [outs[0]]
        return outs

    def far(step, chunk):
        up, down = go(step, chunk, ((2, 0), (2, 1)), ((), ()), (), ((0,), (1,)), step == 0)
        return y_move(up, 1), y_move(down, -1)

    def near(step, chunk, arrived):
        up, down, mine, other = go(
            step,
            chunk,
            ((1, 0), (1, 1), (-1, 0), (-1, 1), (0, 0), (0, 1)),
            (((0, 0),), (), (), ((1, 0),), (), ()),
            [(t, chunk[0]) for t in arrived],
            ((0, 1), (2, 3), (4,), (5,)),
        )
        return y_move(up, 1), y_move(down, -1), mine, other

    def follow(kernel, ins, outs, width, into=None):
        results = by_columns(kernel, ins, outs, width, tuple(last), into)
        last[:] = [results[0]]
        return results

    def across(chunk, sums):
        up, down, mine, other = sums
        return follow(
            give_kernel,
            [(mine, 0), (up, 0), (down, 0), (other, 0), (up, 0, 1), (down, 0, 1)],
            [(chunk[1], 0, f32), (chunk[1], 0, bf16)],
            chunk[1],
        )

    def first_step(chunk, total, give):
        column, width = chunk
        return follow(
            first_kernel,
            [(t, column) for t in (weight, first, second)] + [(total, 0), (z_swap(give), 0)],
            [(width, 0, f32), (width, 0, f32), (width, 0, bf16)],
            width,
        )

    a, b = CHUNKS
    far_ab = far(0, (0, WIDTH))
    near_a = near(0, a, far_ab)
    far_cd = far(1, (0, WIDTH))
    sums_a = across(a, near_a)
    near_b = near(0, b, far_ab)
    near_c = near(1, a, far_cd)
    sums_b = across(b, near_b)
    state_a = first_step(a, *sums_a)
    near_d = near(1, b, far_cd)
    state_b = first_step(b, *sums_b)
    total_c, give_c = across(a, near_c)
    total_d, give_d = across(b, near_d)
    return lax.switch(
        step_index[0] % LEVELS,
        [partial(ending, level) for level in range(LEVELS)],
        state_a,
        state_b,
        total_c,
        total_d,
        z_swap(give_c),
        give_d,
    )


def ending(level, state_a, state_b, total_c, total_d, got_c, give_d):
    distances = 1 << level, 1 << ((level + 1) % LEVELS)
    bf16, f32 = jnp.bfloat16, jnp.float32
    partners = [group_move(state[2], distances[0]) for state in (state_a, state_b)]
    gots = got_c, z_swap(give_d)
    moments, after, boths = None, (), []
    for chunk, state, partner, total, got in zip(
        CHUNKS, (state_a, state_b), partners, (total_c, total_d), gots
    ):
        column, width = chunk
        m, v, u = state
        u, moments = by_columns(
            second_kernel,
            [(t, 0) for t in (u, partner, m, v, total, got)],
            [(width, 0, bf16), (WIDTH, column, f32)],
            width,
            after,
            moments,
        )
        after = (u,)
        boths.append((u, group_move(u, distances[1])))
    weights = None
    for (column, width), both in zip(CHUNKS, boths):
        (weights,) = by_columns(
            average_kernel, [(t, 0) for t in both], [(WIDTH, column, bf16)], width, after, weights
        )
        after = ()
    return weights[None], moments[None]


def solution(mesh):
    in_specs = (
        P(None, "group", "fsdp", None),
        P(None, "group", "fsdp", None),
        P("group", "fsdp", None),
        P("group", "fsdp", None),
        P("group", "fsdp", None),
        P(),
    )
    out_specs = (P("group", "fsdp", None), P("group", "fsdp", None))
    return jax.shard_map(
        per_device, mesh=mesh, in_specs=in_specs, out_specs=out_specs, check_vma=False
    )
```
